256 devices in a mesh: lon: 32 (over z, x_lo, core), lat: 8 (over x_hi, y).
Axes of the slice: x: 4 (x_hi: 2, x_lo: 2; x = x_hi * 2 + x_lo), y: 4, z: 8, core: 2. Of those that a mesh axis runs over, the one named last changes fastest.
Arguments:
- tracer: float32 [2, 2, 2048, 4096], P(None, None, 'lat', 'lon'), may hold values from -6 to 6
- transport: float32 [2, 2, 2048, 4096], P(None, None, 'lat', 'lon'), may hold values from -0.15 to 0.15
- diffusion: float32 [2, 2048, 4096], P(None, 'lat', 'lon'), may hold values from 0.01 to 0.06
- inverse_volume: float32 [2048, 4096], P('lat', 'lon'), may hold values from 0.5 to 2
- sea_mask: int32 [2048, 4096], P('lat', 'lon'), may hold values from 0 to 1, as said below
- regime: int32 [2, 2048, 4096], P(None, 'lat', 'lon'), may hold values from 0 to 2
Outputs:
- tracer_next: float32 [2, 2, 2048, 4096], P(None, None, 'lat', 'lon')
The draws below stay inside these ranges and needn't reach their ends.
Inputs may be any that keep to these rules, and one draw needn't show every extreme that they name: `sea_mask`: the lowest 256 // 2 rows of the grid are land; above them about one cell in eight is land.
All inputs are finite; a program needn't handle non-finite values.
Results may differ from the reference program's by a relative error of at most 0.0003.
Values sent between devices are 32-bit elements; how exact they have to be, the bound alone decides.
A program may use at most 64 MiB of HBM per device.

```python
import math
import jax
import jax.numpy as jnp
from jax import lax

CY = 256
TRACERS = 2
LEVELS = 2
STEPS = 2
NX = 4096
NY = 2048


def draw_sea_mask(key, part):
    key = jax.random.fold_in(key, 7)
    south_band = CY // 2
    row_index = lax.broadcasted_iota(jnp.int32, (NY, NX), 0)
    island_draw = jax.random.randint(key, (NY, NX), 0, 8)
    return jnp.where((row_index >= south_band) & (island_draw > 0), 1, 0).astype(jnp.int32)


def set_ends(entries, rng, low, largest):
    extent = entries.shape
    index_at = [jax.random.randint(jax.random.fold_in(rng, axis), (), 0, extent[axis]) for axis in range(len(extent))]
    entries = entries.at[tuple(index_at)].set(low)
    longest = extent.index(max(extent))
    index_at[longest] = (index_at[longest] + 1) % extent[longest]
    return entries.at[tuple(index_at)].set(largest)


def levels(own_key, extent, pieces, smallest, high):
    def one(dim, blocks):
        heights = jax.random.uniform(jax.random.fold_in(jax.random.fold_in(own_key, 6), dim), (blocks,), jnp.float32, smallest / len(pieces), high / len(pieces))
        return jnp.repeat(jnp.exp(heights), extent[dim] // blocks).reshape((-1,) + (1,) * (len(extent) - dim - 1))

    gain = one(*pieces[0])
    for cut in pieces[1:]:
        gain = gain * one(*cut)
    return gain


def scatter_about(rng, extent, spread, most, split=(), held_as=jnp.bfloat16):
    factor_of = levels(rng, extent, split, -0.22, 0.18) if split else 1.0
    result = jax.random.normal(rng, extent, jnp.float32) * spread * factor_of
    return jnp.minimum(jnp.maximum(result, -most), most).astype(held_as)


def setup_inputs(seed: int = 0) -> dict:
    key_list = jax.random.split(jax.random.key(seed), 7)
    tracer = scatter_about(key_list[0], (TRACERS, LEVELS, NY, NX), 1.0, 6.0, ((2, 8), (3, 32)), jnp.float32)
    transport = jnp.clip(jax.random.uniform(key_list[1], (2, LEVELS, NY, NX), jnp.float32, -0.15, 0.15) * levels(key_list[1], (2, LEVELS, NY, NX), ((2, 8), (3, 32)), -0.4, 0.0), -0.15, 0.15)
    diffusion = jnp.clip(jnp.exp(math.log(0.06) - 1.7917595 * jax.random.uniform(key_list[2], (2, NY, NX), jnp.float32) ** levels(key_list[2], (2, NY, NX), ((1, 8), (2, 32)), -0.2, 0.2)), 0.01, 0.06)
    inverse_volume = jnp.clip(jnp.exp(math.log(2.0) - 1.3862944 * jax.random.uniform(key_list[3], (NY, NX), jnp.float32) ** levels(key_list[3], (NY, NX), ((0, 8), (1, 32)), -0.2, 0.2)), 0.5, 2.0)
    sea_mask = draw_sea_mask(jax.random.fold_in(key_list[6], 71), 0)
    regime = set_ends(jax.random.randint(key_list[5], (2, NY, NX), 0, 3), jax.random.fold_in(key_list[5], 1), 0, 2).astype(jnp.int32)
    return {"tracer": tracer, "transport": transport, "diffusion": diffusion, "inverse_volume": inverse_volume, "sea_mask": sea_mask, "regime": regime}


def minmod(former, latter):
    smaller = jnp.where(jnp.abs(former) < jnp.abs(latter), former, latter)
    return jnp.where(former * latter > 0.0, smaller, jnp.zeros_like(smaller))


def face_flux(behind, current, following, beyond, velocity, regime_face, conduct, opened):
    plus_side = current + 0.5 * minmod(following - current, current - behind)
    minus_side = following + 0.5 * minmod(current - following, following - beyond)
    forward = velocity > 0.0
    limited = jnp.where(forward, plus_side, minus_side)
    upwind = jnp.where(forward, current, following)
    centred = 0.5 * (current + following)
    value = jnp.where(regime_face == 0, upwind, jnp.where(regime_face == 1, centred, limited))
    return opened * (velocity * value - conduct * (following - current))


def extend_grid(field):
    row_count = field.shape[-2]
    lon_ext = jnp.concatenate([field[..., -2:], field, field[..., :2]], axis=-1)
    fold_rows = jnp.stack([field[..., row_count - 1, ::-1], field[..., row_count - 2, ::-1]], axis=-2)
    lat_ext = jnp.concatenate([jnp.zeros_like(field[..., :2, :]), field, fold_rows], axis=-2)
    return lon_ext, lat_ext


def tendency(field, ocean, transport, diffusion, regime, inverse_volume):
    masked = field * ocean
    row_count = masked.shape[-2]
    column_count = masked.shape[-1]
    lon_ext, lat_ext = extend_grid(masked)
    lon_mask, lat_mask = extend_grid(ocean)
    east = face_flux(lon_ext[..., 1:column_count + 1], lon_ext[..., 2:column_count + 2],
                     lon_ext[..., 3:column_count + 3], lon_ext[..., 4:column_count + 4],
                     transport[0], regime[0], diffusion[0],
                     lon_mask[:, 2:column_count + 2] * lon_mask[:, 3:column_count + 3])
    north = face_flux(lat_ext[..., 1:row_count + 1, :], lat_ext[..., 2:row_count + 2, :],
                      lat_ext[..., 3:row_count + 3, :], lat_ext[..., 4:row_count + 4, :],
                      transport[1], regime[1], diffusion[1],
                      lat_mask[2:row_count + 2, :] * lat_mask[3:row_count + 3, :])
    west = jnp.roll(east, 1, axis=-1)
    south = jnp.concatenate([jnp.zeros_like(north[..., :1, :]), north[..., :-1, :]], axis=-2)
    return inverse_volume * ((west - east) + (south - north))


def reference(tracer, transport, diffusion, inverse_volume, sea_mask, regime):
    ocean = sea_mask.astype(jnp.float32)

    def advance(field):
        for step_index in range(STEPS):
            masked = field * ocean
            predictor = ocean * (masked + tendency(masked, ocean, transport, diffusion, regime, inverse_volume))
            change = tendency(predictor, ocean, transport, diffusion, regime, inverse_volume)
            field = ocean * (0.5 * (masked + predictor) + 0.5 * change)
        return field

    return lax.map(advance, tracer)
```

```python
import functools

import jax
import jax.numpy as jnp
from jax import lax
from jax.experimental import pallas as pl
from jax.experimental.pallas import tpu as pltpu
from jax.sharding import PartitionSpec as P

STEPS = 2
MESH = pl.DeviceIdType.MESH
HALO = 8
ROWS = 256
LANES = 128
CHANNELS = 4
F32 = jnp.float32

EAST, NORTH = 0, 3


def iota(rows, axis):
    return lax.broadcasted_iota(jnp.int32, (rows, LANES), axis)


def lanes(tile, index):
    return jnp.take_along_axis(tile, index, axis=1, mode="promise_in_bounds")


def sublanes(tile, index):
    return jnp.take_along_axis(tile, index, axis=0, mode="promise_in_bounds")


def lanes_of(rows, index):
    tiles = [lanes(rows[8 * i : 8 * i + 8], index) for i in range(rows.shape[0] // 8)]
    return tiles[0] if len(tiles) == 1 else jnp.concatenate(tiles, axis=0)


def face_flux(cell, gap, gap_behind, gap_beyond, a, b, c):
    other = jnp.where(a > 0.0, gap_behind, gap_beyond)
    slope = jnp.maximum(jnp.minimum(gap, 0.0), jnp.minimum(other, jnp.maximum(gap, 0.0)))
    return a * cell + b * gap + c * slope


def face_coefficients(velocity, conduct, regime, opened):
    a = opened * velocity
    share = jnp.where(regime == 1.0, 0.5, jnp.where(velocity > 0.0, 0.0, 1.0))
    b = a * share - opened * conduct
    c = jnp.where(regime == 2.0, 0.5 * jnp.abs(a), 0.0)
    return a, b, c


def stage(source, target, kept, planes, north_flux, start, count, channels, levels):
    volume = planes[6 * levels, pl.ds(start, count)]
    for ch in range(channels):
        level = 6 * (ch % levels)

        def plane(i):
            return planes[level + i, pl.ds(start, count)]

        cell = source[ch, pl.ds(start, count)]
        behind = source[ch, pl.ds(start - 1, count)]
        ahead = source[ch, pl.ds(start + 1, count)]
        beyond = source[ch, pl.ds(start + 2, count)]
        north = face_flux(
            cell, ahead - cell, cell - behind, beyond - ahead, plane(3), plane(4), plane(5)
        )
        north_flux[ch, pl.ds(start, count)] = north
        gap = pltpu.roll(cell, LANES - 1, 1) - cell
        east = face_flux(
            cell,
            gap,
            pltpu.roll(gap, 1, 1),
            pltpu.roll(gap, LANES - 1, 1),
            plane(0),
            plane(1),
            plane(2),
        )
        west = pltpu.roll(east, 1, 1)
        south = north_flux[ch, pl.ds(start - 1, count)]
        change = volume * ((west - east) + (south - north))
        if kept is None:
            target[ch, pl.ds(start, count)] = cell + change
        else:
            target[ch, pl.ds(start, count)] = 0.5 * ((kept[ch, pl.ds(start, count)] + cell) + change)


def fold_fix(source, target, planes, second, row, channels, levels, factor):
    first_row = iota(8, 0) == 0
    for ch in range(channels):
        level = 6 * (ch % levels)
        extra = 3 * (ch % levels)
        cell = source[ch, pl.ds(row - 1, 8)]
        behind = source[ch, pl.ds(row - 2, 8)]
        ahead = source[ch, pl.ds(row, 8)]
        beyond = source[ch, pl.ds(row + 1, 8)]
        gaps = (cell, ahead - cell, cell - behind, beyond - ahead)
        mine = face_flux(*gaps, *[planes[level + 3 + i, pl.ds(row - 1, 8)] for i in range(3)])
        theirs = face_flux(*gaps, *[second[extra + i] for i in range(3)])
        volume = planes[6 * levels, pl.ds(row, 8)]
        fix = jnp.where(first_row, volume * (theirs - mine), 0.0)
        target[ch, pl.ds(row, 8)] = target[ch, pl.ds(row, 8)] + factor * fix


def kernel(
    lon_count,
    lat_count,
    tracer,
    transport,
    diffusion,
    inverse_volume,
    sea_mask,
    regime,
    out,
    in_tracer,
    in_transport,
    in_diffusion,
    in_volume,
    in_mask,
    in_regime,
    far_tracer,
    far_transport,
    far_diffusion,
    far_volume,
    far_mask,
    far_regime,
    mask,
    field,
    guess,
    planes,
    flux,
    packs,
    edges,
    lat_mask,
    lat_field,
    lat_guess,
    lat_planes,
    lat_flux,
    lat_up,
    lat_second,
    lon_raw,
    lon_field,
    lon_guess,
    lon_planes,
    lon_flux,
    lon_second_raw,
    lon_second,
    load_sem,
    lat_send,
    lat_recv,
    lon_send,
    lon_recv,
    corner_send,
    corner_recv,
):
    lon = lax.axis_index("lon")
    lat = lax.axis_index("lat")
    top = lat == lat_count - 1
    bottom = lat == 0
    left = lax.rem(lon + lon_count - 1, lon_count)
    right = lax.rem(lon + 1, lon_count)
    up = jnp.where(top, lat, lat + 1)
    up_lon = jnp.where(top, lon_count - 1 - lon, lon)
    up_left = jnp.where(top, lax.rem(lon_count - lon, lon_count), left)
    up_right = jnp.where(top, lax.rem(2 * lon_count - 2 - lon, lon_count), right)
    self_left = jnp.logical_and(top, up_left == lon)
    self_right = jnp.logical_and(top, up_right == lon)
    down = jnp.where(bottom, lat, lat - 1)

    barrier = pltpu.get_barrier_semaphore()

    def greet(to_lon, to_lat):
        pl.semaphore_signal(
            barrier, inc=1, device_id={"lon": to_lon, "lat": to_lat}, device_id_type=MESH
        )

    greet(left, lat)
    greet(right, lat)
    greet(up_lon, up)

    @pl.when(jnp.logical_not(self_left))
    def _():
        greet(up_left, up)

    @pl.when(jnp.logical_not(self_right))
    def _():
        greet(up_right, up)

    @pl.when(jnp.logical_not(bottom))
    def _():
        greet(lon, down)
        greet(left, down)
        greet(right, down)

    arrays = (tracer, transport, diffusion, inverse_volume, sea_mask, regime)
    held = (in_tracer, in_transport, in_diffusion, in_volume, in_mask, in_regime)
    landing = (far_tracer, far_transport, far_diffusion, far_volume, far_mask, far_regime)
    loads = [pltpu.make_async_copy(a, h, load_sem.at[i]) for i, (a, h) in enumerate(zip(arrays, held))]
    for load in loads:
        load.start()

    pad = jnp.zeros((8, LANES), F32)
    for ref, last in ((field, ROWS), (guess, ROWS), (flux, ROWS), (planes, ROWS)):
        for i in range(ref.shape[0]):
            ref[i, pl.ds(0, 8)] = pad
            ref[i, pl.ds(8 + last, 8)] = pad
    mask[pl.ds(ROWS + 8, 8)] = pad
    for ref, last in ((lat_field, 48), (lat_guess, 48), (lat_flux, 48)):
        for i in range(ref.shape[0]):
            ref[i, pl.ds(0, 8)] = pad
            ref[i, pl.ds(8 + last, 8)] = pad
    for ref in (lon_field, lon_guess, lon_flux):
        for i in range(2):
            ref[i, 0, pl.ds(0, 8)] = pad
            ref[i, 0, pl.ds(8 + ROWS + 16, 8)] = pad
    lat_mask[pl.ds(56, 8)] = pad
    for i in range(2):
        lon_raw[i, 6, pl.ds(ROWS + 16, 8)] = pad

    @pl.when(bottom)
    def _():
        for ref in landing:
            ref[0] = jnp.zeros(ref.shape[1:], ref.dtype)
        for i in range(2):
            edges[i, pl.ds(0, 8)] = pad

    for load in loads:
        load.wait()

    def pack(i, carry):
        n = 64
        r = pl.multiple_of(i * n, n)
        rows, padded = pl.ds(r, n), pl.ds(pl.multiple_of(r + 8, 8), n)
        group = iota(n, 1) >> 3
        sea = in_mask[rows].astype(F32)
        mask[padded] = sea
        volume = in_volume[rows] * sea
        planes[12, padded] = volume
        cells = []
        for ch in range(CHANNELS):
            cell = in_tracer[ch // 2, ch % 2, rows] * sea
            field[ch, padded] = cell
            cells.append(cell)
        cells += [in_transport[j // 2, j % 2, rows] for j in range(4)]
        cells += [in_diffusion[j, rows] for j in range(2)]
        cells += [volume, sea]
        cells += [in_regime[j, rows].astype(F32) for j in range(2)]
        west_pack = east_pack = cells[0]
        for k in range(1, 14):
            moved = pltpu.roll(cells[k], 8 * k, 1)
            west_pack = jnp.where(group == k, moved, west_pack)
            east_pack = jnp.where(group == k - 1, moved, east_pack)
        east_pack = jnp.where(group == 15, cells[0], east_pack)
        packs[0, rows] = west_pack
        packs[1, rows] = east_pack
        return carry

    lax.fori_loop(0, 4, pack, 0)

    pl.semaphore_wait(
        barrier,
        5
        - self_left.astype(jnp.int32)
        - self_right.astype(jnp.int32)
        + 3 * jnp.logical_not(bottom).astype(jnp.int32),
    )

    def remote(src, dst, send, recv, to_lon, to_lat):
        return pltpu.make_async_remote_copy(
            src_ref=src,
            dst_ref=dst,
            send_sem=send,
            recv_sem=recv,
            device_id={"lon": to_lon, "lat": to_lat},
            device_id_type=MESH,
        )

    def row_slice(ref, start):
        return ref.at[(slice(None),) * (len(ref.shape) - 2) + (pl.ds(start, 8),)]

    to_left = remote(packs.at[0], edges.at[1, pl.ds(8, ROWS)], lon_send.at[0], lon_recv.at[1], left, lat)
    to_right = remote(packs.at[1], edges.at[0, pl.ds(8, ROWS)], lon_send.at[1], lon_recv.at[0], right, lat)
    corner_row = pl.multiple_of(jnp.where(top, ROWS + 8, 0), 8)
    top_int = top.astype(jnp.int32)
    corner_ul = remote(
        packs.at[0, pl.ds(ROWS - 8, 8)],
        edges.at[1 - top_int, pl.ds(corner_row, 8)],
        corner_send.at[0],
        corner_recv.at[1 + top_int],
        up_left,
        up,
    )
    corner_ur = remote(
        packs.at[1, pl.ds(ROWS - 8, 8)],
        edges.at[top_int, pl.ds(corner_row, 8)],
        corner_send.at[1],
        corner_recv.at[3 * top_int],
        up_right,
        up,
    )
    corner_dl = remote(
        packs.at[0, pl.ds(0, 8)],
        edges.at[1, pl.ds(ROWS + 8, 8)],
        corner_send.at[2],
        corner_recv.at[3],
        left,
        down,
    )
    corner_dr = remote(
        packs.at[1, pl.ds(0, 8)],
        edges.at[0, pl.ds(ROWS + 8, 8)],
        corner_send.at[3],
        corner_recv.at[2],
        right,
        down,
    )
    to_up = [
        remote(row_slice(a, ROWS - 8), f.at[top_int], lat_send.at[0, i], lat_recv.at[top_int, i], up_lon, up)
        for i, (a, f) in enumerate(zip(arrays, landing))
    ]
    to_down = [
        remote(row_slice(a, 0), f.at[1], lat_send.at[1, i], lat_recv.at[1, i], lon, down)
        for i, (a, f) in enumerate(zip(arrays, landing))
    ]
    to_left.start()
    to_right.start()

    @pl.when(jnp.logical_not(self_left))
    def _():
        corner_ul.start()

    @pl.when(jnp.logical_not(self_right))
    def _():
        corner_ur.start()

    for copy in to_up:
        copy.start()

    @pl.when(jnp.logical_not(bottom))
    def _():
        corner_dl.start()
        corner_dr.start()
        for copy in to_down:
            copy.start()

    @pl.when(self_left)
    def _():
        edges[0, pl.ds(ROWS + 8, 8)] = packs[0, pl.ds(ROWS - 8, 8)]

    @pl.when(self_right)
    def _():
        edges[1, pl.ds(ROWS + 8, 8)] = packs[1, pl.ds(ROWS - 8, 8)]

    lane, row8 = iota(8, 1), iota(8, 0)
    slot, place = lane >> 5, lane & 31
    odd = slot & 1
    own_index = (jnp.maximum(place - 8, 0), jnp.minimum(place + 104, LANES - 1))
    own_lane = (place >= 8, place < 24)
    pack_slot = [slot, 4 + odd, 6 + odd] + [jnp.full_like(slot, k) for k in range(8, 14)]

    def unpack_index(side, a):
        at = pack_slot[a] if side == 1 else (pack_slot[a] + 15) & 15
        return 8 * at + (lane & 7)

    def own_strips(side, fourteen):
        index = own_index[side]
        n = fourteen[0].shape[0]
        wide_slot, wide_odd = iota(n, 1) >> 5, (iota(n, 1) >> 5) & 1
        got = [lanes_of(a, index) for a in fourteen]
        cell = got[0]
        for ch in range(1, CHANNELS):
            cell = jnp.where(wide_slot == ch, got[ch], cell)
        speed_east = jnp.where(wide_odd == 1, got[5], got[4])
        speed_north = jnp.where(wide_odd == 1, got[7], got[6])
        return [cell, speed_east, speed_north] + got[8:]

    def prepare(i, carry):
        n = 64
        r = pl.multiple_of(i * n, n)
        rows, padded = pl.ds(r, n), pl.ds(pl.multiple_of(r + 8, 8), n)
        sea = mask[padded]
        open_east = sea * pltpu.roll(sea, LANES - 1, 1)
        open_north = sea * mask[pl.ds(r + 9, n)]
        regimes = [in_regime[j, rows].astype(F32) for j in range(2)]
        for level in range(2):
            for way, opened in ((0, open_east), (1, open_north)):
                found = face_coefficients(
                    in_transport[way, level, rows], in_diffusion[way, rows], regimes[way], opened
                )
                for j in range(3):
                    planes[6 * level + 3 * way + j, padded] = found[j]
        return carry

    lax.fori_loop(0, 4, prepare, 0)

    def strips(i, carry):
        n = 32
        r = pl.multiple_of(i * n, n)
        rows, padded = pl.ds(r, n), pl.ds(pl.multiple_of(r + 8, 8), n)
        fourteen = [field[ch, padded] for ch in range(CHANNELS)]
        fourteen += [in_transport[j // 2, j % 2, rows] for j in range(4)]
        fourteen += [in_diffusion[j, rows] for j in range(2)]
        fourteen += [planes[12, padded], mask[padded]]
        fourteen += [in_regime[j, rows].astype(F32) for j in range(2)]
        for side in range(2):
            for a, strip in enumerate(own_strips(side, fourteen)):
                lon_raw[side, a, padded] = strip
        return carry

    lax.fori_loop(0, 8, strips, 0)

    for ch in range(CHANNELS):
        lat_field[ch, pl.ds(16, 16)] = field[ch, pl.ds(8, 16)]
        lat_field[ch, pl.ds(32, 16)] = field[ch, pl.ds(ROWS - 8, 16)]
    for i in range(13):
        lat_planes[i, pl.ds(16, 16)] = planes[i, pl.ds(8, 16)]
        lat_planes[i, pl.ds(32, 16)] = planes[i, pl.ds(ROWS - 8, 16)]
    lat_mask[pl.ds(16, 16)] = mask[pl.ds(8, 16)]
    lat_mask[pl.ds(32, 16)] = mask[pl.ds(ROWS - 8, 16)]

    def interior(step, carry):
        def predict(i, c):
            stage(field, guess, None, planes, flux, pl.multiple_of(i * 32 + 8, 8), 32, CHANNELS, 2)
            return c

        def correct(i, c):
            stage(guess, field, field, planes, flux, pl.multiple_of(i * 32 + 8, 8), 32, CHANNELS, 2)
            return c

        lax.fori_loop(0, 8, predict, 0)
        lax.fori_loop(0, 8, correct, 0)
        return carry

    lax.fori_loop(0, STEPS, interior, 0)

    for i, f in enumerate(landing):
        remote(f.at[1], f.at[1], lat_send.at[0, i], lat_recv.at[1, i], lon, lat).wait_recv()

    @pl.when(jnp.logical_not(bottom))
    def _():
        for i, f in enumerate(landing):
            remote(f.at[0], f.at[0], lat_send.at[0, i], lat_recv.at[0, i], lon, lat).wait_recv()
        for side in range(2):
            remote(
                edges.at[side, pl.ds(0, 8)], edges.at[side, pl.ds(0, 8)], corner_send.at[0],
                corner_recv.at[side], lon, lat,
            ).wait_recv()

    @pl.when(jnp.logical_not(self_left))
    def _():
        remote(
            edges.at[0, pl.ds(ROWS + 8, 8)], edges.at[0, pl.ds(ROWS + 8, 8)], corner_send.at[0],
            corner_recv.at[2], lon, lat,
        ).wait_recv()

    @pl.when(jnp.logical_not(self_right))
    def _():
        remote(
            edges.at[1, pl.ds(ROWS + 8, 8)], edges.at[1, pl.ds(ROWS + 8, 8)], corner_send.at[0],
            corner_recv.at[3], lon, lat,
        ).wait_recv()

    def prepared(side):
        sea = far_mask[side].astype(F32)
        tiles = [far_tracer[side, ch // 2, ch % 2] * sea for ch in range(CHANNELS)]
        tiles += [far_transport[side, j // 2, j % 2] for j in range(4)]
        tiles += [far_diffusion[side, j] for j in range(2)]
        tiles += [far_volume[side] * sea, sea]
        tiles += [far_regime[side, j].astype(F32) for j in range(2)]
        return tiles

    below = prepared(0)
    for side in range(2):
        for a, strip in enumerate(own_strips(side, below)):
            lon_raw[side, a, pl.ds(0, 8)] = strip

    @pl.when(jnp.logical_not(top))
    def _():
        above = prepared(1)
        for k, tile in enumerate(above):
            lat_up[k] = tile
        for side in range(2):
            for a, strip in enumerate(own_strips(side, above)):
                lon_raw[side, a, pl.ds(ROWS + 8, 8)] = strip

    row_cell, row_north = 7 - row8, jnp.maximum(6 - row8, 0)

    @pl.when(top)
    def _():
        across = prepared(1)
        lane_cell, lane_east = LANES - 1 - lane, jnp.maximum(LANES - 2 - lane, 0)
        for k, tile in enumerate(across):
            east, north = k in (4, 5, 8, 12), k in (6, 7, 9, 13)
            turned = lanes(tile, lane_east if east else lane_cell)
            if k in (4, 5, 6, 7):
                turned = -turned
            lat_up[k] = sublanes(turned, row_north if north else row_cell)
            if north:
                lat_up[14 + (6, 7, 9, 13).index(k)] = sublanes(turned, row_cell)
        slot_cell, slot_east = lane ^ 31, 32 * slot + jnp.maximum(30 - place, 0)
        for side in range(2):
            whole = own_strips(1 - side, across)
            corner = edges[side, pl.ds(ROWS + 8, 8)]
            for a, strip in enumerate(whole):
                strip = jnp.where(own_lane[1 - side], strip, lanes(corner, unpack_index(1 - side, a)))
                east, north = a in (1, 3, 7), a in (2, 4, 8)
                turned = lanes(strip, slot_east if east else slot_cell)
                if a in (1, 2):
                    turned = -turned
                lon_raw[side, a, pl.ds(ROWS + 8, 8)] = sublanes(turned, row_north if north else row_cell)
                if north:
                    lon_second_raw[side, (2, 4, 8).index(a)] = sublanes(turned, row_cell)

    lat_mask[pl.ds(8, 8)] = below[11]
    lat_mask[pl.ds(48, 8)] = lat_up[11]
    for ch in range(CHANNELS):
        lat_field[ch, pl.ds(8, 8)] = below[ch]
        lat_field[ch, pl.ds(48, 8)] = lat_up[ch]
    lat_planes[12, pl.ds(8, 8)] = below[10]
    lat_planes[12, pl.ds(48, 8)] = lat_up[10]
    highest = [None] * 4 + [in_transport[j // 2, j % 2, pl.ds(ROWS - 8, 8)] for j in range(4)]
    highest += [in_diffusion[j, pl.ds(ROWS - 8, 8)] for j in range(2)] + [None, None]
    highest += [in_regime[j, pl.ds(ROWS - 8, 8)].astype(F32) for j in range(2)]
    upper = [lat_up[k] for k in range(14)]
    for at, tiles in ((8, below), (40, highest), (48, upper)):
        sea = lat_mask[pl.ds(at, 8)]
        opened = (sea * pltpu.roll(sea, LANES - 1, 1), sea * lat_mask[pl.ds(at + 1, 8)])
        for level in range(2):
            for way in range(2):
                found = face_coefficients(
                    tiles[4 + 2 * way + level], tiles[8 + way], tiles[12 + way], opened[way]
                )
                for j in range(3):
                    lat_planes[6 * level + 3 * way + j, pl.ds(at, 8)] = found[j]

    for side in range(2):
        remote(
            edges.at[side, pl.ds(8, ROWS)], edges.at[side, pl.ds(8, ROWS)], lon_send.at[0],
            lon_recv.at[side], lon, lat,
        ).wait_recv()

    def join(i, carry):
        n = 136
        r = pl.multiple_of(i * n, 8)
        rows, padded = pl.ds(r, n), pl.ds(pl.multiple_of(r + 8, 8), n)
        wide_place = iota(n, 1) & 31
        whole = jnp.logical_and(iota(n, 0) + r >= ROWS + 8, top)
        for side in range(2):
            own = jnp.logical_or(wide_place >= 8 if side == 0 else wide_place < 24, whole)
            edge = edges[side, rows]
            for a in range(9):
                strip = jnp.where(own, lon_raw[side, a, rows], lanes_of(edge, unpack_index(side, a)))
                if a == 0:
                    lon_field[side, 0, padded] = strip
                elif a == 5:
                    lon_planes[side, 6, padded] = strip
                else:
                    lon_raw[side, a, rows] = strip
        return carry

    lax.fori_loop(0, 2, join, 0)

    def lon_coefficients(i, carry):
        n = 136
        r = pl.multiple_of(i * n, 8)
        rows, padded = pl.ds(r, n), pl.ds(pl.multiple_of(r + 8, 8), n)
        for side in range(2):
            sea = lon_raw[side, 6, rows]
            opened = (sea * pltpu.roll(sea, LANES - 1, 1), sea * lon_raw[side, 6, pl.ds(r + 1, n)])
            for way in range(2):
                found = face_coefficients(
                    lon_raw[side, 1 + way, rows],
                    lon_raw[side, 3 + way, rows],
                    lon_raw[side, 7 + way, rows],
                    opened[way],
                )
                for j in range(3):
                    lon_planes[side, 3 * way + j, padded] = found[j]
        return carry

    lax.fori_loop(0, 2, lon_coefficients, 0)

    @pl.when(top)
    def _():
        opened = lat_mask[pl.ds(47, 8)] * lat_mask[pl.ds(48, 8)]
        for level in range(2):
            found = face_coefficients(lat_up[14 + level], lat_up[16], lat_up[17], opened)
            for j in range(3):
                lat_second[3 * level + j] = found[j]
        for side in range(2):
            opened = lon_raw[side, 6, pl.ds(ROWS + 7, 8)] * lon_raw[side, 6, pl.ds(ROWS + 8, 8)]
            found = face_coefficients(*[lon_second_raw[side, j] for j in range(3)], opened)
            for j in range(3):
                lon_second[side, j] = found[j]

    def rim(step, carry):
        for source, target, kept, factor in ((0, 1, None, 1.0), (1, 0, 0, 0.5)):
            lat_pair = (lat_field, lat_guess)
            stage(
                lat_pair[source], lat_pair[target], None if kept is None else lat_field,
                lat_planes, lat_flux, 8, 48, CHANNELS, 2,
            )
            for side in range(2):
                pair = (lon_field.at[side], lon_guess.at[side])
                stage(
                    pair[source], pair[target], None if kept is None else pair[0],
                    lon_planes.at[side], lon_flux.at[side], 8, ROWS + 16, 1, 1,
                )

            @pl.when(top)
            def _():
                fold_fix(lat_pair[source], lat_pair[target], lat_planes, lat_second, 48, CHANNELS, 2, factor)
                for side in range(2):
                    pair = (lon_field.at[side], lon_guess.at[side])
                    fold_fix(
                        pair[source], pair[target], lon_planes.at[side], lon_second.at[side],
                        ROWS + 16, 1, 1, factor,
                    )

        return carry

    lax.fori_loop(0, STEPS, rim, 0)

    for ch in range(CHANNELS):
        field[ch, pl.ds(8, 8)] = lat_field[ch, pl.ds(16, 8)]
        field[ch, pl.ds(ROWS, 8)] = lat_field[ch, pl.ds(40, 8)]

    def finish(i, carry):
        n = 64
        r = pl.multiple_of(i * n, n)
        rows, padded = pl.ds(r, n), pl.ds(pl.multiple_of(r + 8, 8), n)
        deep = pl.ds(pl.multiple_of(r + 16, 8), n)
        wide = iota(n, 1)
        both = jnp.where((wide & 31) < 16, lon_field[0, 0, deep], lon_field[1, 0, deep])
        inner = jnp.logical_and(wide >= 8, wide < LANES - 8)
        for ch in range(CHANNELS):
            index = 32 * ch + (lane & 7) + jnp.where(lane < 64, 8, 16)
            out[ch // 2, ch % 2, rows] = jnp.where(inner, field[ch, padded], lanes_of(both, index))
        return carry

    lax.fori_loop(0, 4, finish, 0)

    to_left.wait_send()
    to_right.wait_send()
    for copy in to_up:
        copy.wait_send()

    @pl.when(jnp.logical_not(self_left))
    def _():
        corner_ul.wait_send()

    @pl.when(jnp.logical_not(self_right))
    def _():
        corner_ur.wait_send()

    @pl.when(jnp.logical_not(bottom))
    def _():
        corner_dl.wait_send()
        corner_dr.wait_send()
        for copy in to_down:
            copy.wait_send()


def solution(mesh):
    lon_count, lat_count = mesh.shape["lon"], mesh.shape["lat"]
    placed = (
        P(None, None, "lat", "lon"),
        P(None, None, "lat", "lon"),
        P(None, "lat", "lon"),
        P("lat", "lon"),
        P("lat", "lon"),
        P(None, "lat", "lon"),
    )

    def local(*arrays):
        shapes = [a.shape for a in arrays]
        types = [a.dtype for a in arrays]
        far = [(2,) + s[:-2] + (8, LANES) for s in shapes]
        tall, wide = ROWS + 16, ROWS + 32

        def vmem(*shape):
            return pltpu.VMEM(shape, F32)

        return pl.pallas_call(
            functools.partial(kernel, lon_count, lat_count),
            out_shape=pltpu.VMEM(shapes[0], F32),
            in_specs=[pl.BlockSpec(memory_space=pl.ANY)] * 6,
            out_specs=pl.BlockSpec(memory_space=pltpu.VMEM),
            scratch_shapes=[
                *[pltpu.VMEM(s, t) for s, t in zip(shapes, types)],
                *[pltpu.VMEM(s, t) for s, t in zip(far, types)],
                vmem(tall, LANES),
                vmem(CHANNELS, tall, LANES),
                vmem(CHANNELS, tall, LANES),
                vmem(13, tall, LANES),
                vmem(CHANNELS, tall, LANES),
                vmem(2, ROWS, LANES),
                vmem(2, tall, LANES),
                vmem(64, LANES),
                vmem(CHANNELS, 64, LANES),
                vmem(CHANNELS, 64, LANES),
                vmem(13, 64, LANES),
                vmem(CHANNELS, 64, LANES),
                vmem(18, 8, LANES),
                vmem(6, 8, LANES),
                vmem(2, 9, tall + 8, LANES),
                vmem(2, 1, wide, LANES),
                vmem(2, 1, wide, LANES),
                vmem(2, 7, wide, LANES),
                vmem(2, 1, wide, LANES),
                vmem(2, 3, 8, LANES),
                vmem(2, 3, 8, LANES),
                pltpu.SemaphoreType.DMA((6,)),
                pltpu.SemaphoreType.DMA((2, 6)),
                pltpu.SemaphoreType.DMA((2, 6)),
                pltpu.SemaphoreType.DMA((2,)),
                pltpu.SemaphoreType.DMA((2,)),
                pltpu.SemaphoreType.DMA((4,)),
                pltpu.SemaphoreType.DMA((4,)),
            ],
            compiler_params=pltpu.CompilerParams(
                collective_id=0, has_side_effects=True, vmem_limit_bytes=40 * 1024 * 1024
            ),
        )(*arrays)

    return jax.shard_map(
        local, mesh=mesh, in_specs=placed, out_specs=P(None, None, "lat", "lon"), check_vma=False
    )
```

```python
import functools

import jax
import jax.numpy as jnp
from jax import lax
from jax.experimental import pallas as pl
from jax.experimental.pallas import tpu as pltpu
from jax.sharding import PartitionSpec as P

STEPS = 2
MESH = pl.DeviceIdType.MESH
HALO = 8
ROWS = 256
LANES = 128
CHANNELS = 4
F32 = jnp.float32
INNER = 256
PACK = 64
JOIN = 136

SENT = 13


def iota(rows, axis):
    return lax.broadcasted_iota(jnp.int32, (rows, LANES), axis)


def lanes(tile, index):
    return jnp.take_along_axis(tile, index, axis=1, mode="promise_in_bounds")


def sublanes(tile, index):
    return jnp.take_along_axis(tile, index, axis=0, mode="promise_in_bounds")


def lanes_of(rows, index):
    tiles = [lanes(rows[8 * i : 8 * i + 8], index) for i in range(rows.shape[0] // 8)]
    return tiles[0] if len(tiles) == 1 else jnp.concatenate(tiles, axis=0)


def face_flux(cell, gap, gap_behind, gap_beyond, a, b, c):
    other = jnp.where(a > 0.0, gap_behind, gap_beyond)
    slope = jnp.maximum(jnp.minimum(gap, 0.0), jnp.minimum(other, jnp.maximum(gap, 0.0)))
    return a * cell + b * gap + c * slope


def face_coefficients(velocity, conduct, regime, opened):
    a = opened * velocity
    share = jnp.where(regime == 1.0, 0.5, jnp.where(velocity > 0.0, 0.0, 1.0))
    b = a * share - opened * conduct
    c = jnp.where(regime == 2.0, 0.5 * jnp.abs(a), 0.0)
    return a, b, c


def stage(source, target, kept, planes, north_flux, start, count, channels, levels, fold=None, patch=None):
    rows = pl.ds(start, count)
    volume = planes[6 * levels, rows]
    results = []
    for ch in range(channels):
        level = 6 * (ch % levels)

        def plane(i):
            return planes[level + i, rows]

        cell = source[ch, rows]
        behind = source[ch, pl.ds(start - 1, count)]
        ahead = source[ch, pl.ds(start + 1, count)]
        beyond = source[ch, pl.ds(start + 2, count)]
        north = face_flux(
            cell, ahead - cell, cell - behind, beyond - ahead, plane(3), plane(4), plane(5)
        )
        north_flux[ch, rows] = north
        if fold is not None:
            second, row = fold
            at = [source[ch, pl.ds(row + i, 8)] for i in (-2, -1, 0, 1)]
            theirs = face_flux(
                at[1],
                at[2] - at[1],
                at[1] - at[0],
                at[3] - at[2],
                *[second[3 * (ch % levels) + i] for i in range(3)],
            )
            north_flux[ch, pl.ds(row - 1, 1)] = theirs[0:1]
        east1 = pltpu.roll(cell, LANES - 1, 1)
        east2 = pltpu.roll(cell, LANES - 2, 1)
        west1 = pltpu.roll(cell, 1, 1)
        east = face_flux(
            cell,
            east1 - cell,
            cell - west1,
            east2 - east1,
            plane(0),
            plane(1),
            plane(2),
        )
        west = pltpu.roll(east, 1, 1)
        south = north_flux[ch, pl.ds(start - 1, count)]
        result = volume * ((west - east) + (south - north))
        if kept is None:
            result = cell + result
        else:
            result = 0.5 * ((kept[ch, rows] + cell) + result)
        if patch is not None:
            result = patch(result)
        target[ch, rows] = result
        results.append(result)
    return results


def kernel(
    lon_count,
    lat_count,
    tracer,
    transport,
    diffusion,
    inverse_volume,
    sea_mask,
    regime,
    out,
    in_tracer,
    in_transport,
    in_diffusion,
    in_volume,
    in_mask,
    in_regime,
    mask,
    field,
    guess,
    planes,
    flux,
    packs,
    edges,
    lat_packs,
    lat_edges,
    lat_mask,
    lat_field,
    lat_guess,
    lat_planes,
    lat_flux,
    lat_up,
    lat_second,
    lon_raw,
    lon_field,
    lon_guess,
    lon_planes,
    lon_flux,
    lon_second,
    patches,
    load_sem,
    lat_send,
    lat_recv,
    lon_send,
    lon_recv,
    corner_send,
    corner_recv,
):
    lon = lax.axis_index("lon")
    lat = lax.axis_index("lat")
    top = lat == lat_count - 1
    bottom = lat == 0
    left = lax.rem(lon + lon_count - 1, lon_count)
    right = lax.rem(lon + 1, lon_count)
    up = jnp.where(top, lat, lat + 1)
    up_lon = jnp.where(top, lon_count - 1 - lon, lon)
    up_left = jnp.where(top, lax.rem(lon_count - lon, lon_count), left)
    up_right = jnp.where(top, lax.rem(2 * lon_count - 2 - lon, lon_count), right)
    self_left = jnp.logical_and(top, up_left == lon)
    self_right = jnp.logical_and(top, up_right == lon)
    down = jnp.where(bottom, lat, lat - 1)

    barrier = pltpu.get_barrier_semaphore()

    def greet(to_lon, to_lat):
        pl.semaphore_signal(
            barrier, inc=1, device_id={"lon": to_lon, "lat": to_lat}, device_id_type=MESH
        )

    @pl.when(jnp.logical_not(self_left))
    def _():
        greet(up_left, up)

    @pl.when(jnp.logical_not(self_right))
    def _():
        greet(up_right, up)

    @pl.when(jnp.logical_not(bottom))
    def _():
        greet(left, down)
        greet(right, down)
        greet(lon, down)

    greet(up_lon, up)
    greet(left, lat)
    greet(right, lat)

    arrays = (tracer, transport, diffusion, inverse_volume, sea_mask, regime)
    held = (in_tracer, in_transport, in_diffusion, in_volume, in_mask, in_regime)
    loads = [pltpu.make_async_copy(a, h, load_sem.at[i]) for i, (a, h) in enumerate(zip(arrays, held))]
    for load in loads:
        load.start()

    pad = jnp.zeros((8, LANES), F32)
    for ref in (field, guess, flux, planes):
        for i in range(ref.shape[0]):
            ref[i, pl.ds(0, 8)] = pad
            ref[i, pl.ds(8 + ROWS, 8)] = pad
    mask[pl.ds(ROWS + 8, 8)] = pad
    for ref in (lat_field, lat_guess, lat_flux):
        for i in range(ref.shape[0]):
            ref[i, pl.ds(0, 8)] = pad
            ref[i, pl.ds(56, 8)] = pad
    for ref in (lon_field, lon_guess, lon_flux):
        ref[0, pl.ds(0, 8)] = pad
        ref[0, pl.ds(24 + ROWS, 8)] = pad
    lat_mask[pl.ds(56, 8)] = pad
    lon_raw[4, pl.ds(ROWS + 16, 8)] = pad
    for i in range(2):
        edges[i, pl.ds(ROWS + 16, 8)] = pad

    @pl.when(bottom)
    def _():
        lat_edges[0] = jnp.zeros(lat_edges.shape[1:], F32)
        for i in range(2):
            edges[i, pl.ds(0, 8)] = pad

    for load in loads:
        load.wait()

    lane, row8 = iota(8, 1), iota(8, 0)
    place, west_side = lane & 7, lane < 64
    own_cell = jnp.where(west_side, place, LANES - 1 - place)
    own_east = jnp.where(
        west_side, place, jnp.where((lane & 15) >= 8, LANES - 2 - place, LANES - 1)
    )
    level_lane = (lane >> 4) & 1
    sent_cell = jnp.where(west_side, LANES - 8 + place, 7 - place)
    sent_east = jnp.where(west_side, LANES - 8 + place, jnp.maximum(6 - place, 0))
    swapped_cell = jnp.where(west_side, 7 - place, LANES - 8 + place)
    swapped_east = jnp.where(west_side, jnp.maximum(6 - place, 0), LANES - 8 + place)

    def reflected(n):
        return jnp.where(iota(n, 1) < 64, 1.0, -1.0)

    def own_strips(cells, moves, steady):
        n = cells[0].shape[0]
        channel, odd = (iota(n, 1) >> 4) & 3, ((iota(n, 1) >> 4) & 1) == 1
        got = [lanes_of(a, own_cell) for a in cells]
        cell = got[0]
        for ch in range(1, CHANNELS):
            cell = jnp.where(channel == ch, got[ch], cell)
        speed_east = [lanes_of(a, own_east) for a in moves[:2]]
        speed_north = [lanes_of(a, own_cell) for a in moves[2:]]
        return cell, [
            jnp.where(odd, speed_east[1], speed_east[0]) * reflected(n),
            jnp.where(odd, speed_north[1], speed_north[0]),
            lanes_of(steady[0], own_east),
            lanes_of(steady[1], own_cell),
            lanes_of(steady[2], own_cell),
            lanes_of(steady[3], own_east),
            lanes_of(steady[4], own_cell),
            lanes_of(steady[2], own_next),
        ]

    own_next = jnp.where(west_side, place + 1, LANES - 2 - place)

    def tile_rows(r, n):
        rows = pl.ds(r, n)
        sea = in_mask[rows].astype(F32)
        cells = [in_tracer[ch // 2, ch % 2, rows] * sea for ch in range(CHANNELS)]
        moves = [in_transport[j // 2, j % 2, rows] for j in range(4)]
        steady = [in_diffusion[j, rows] for j in range(2)]
        steady += [in_volume[rows] * sea]
        steady += [in_regime[j, rows].astype(F32) for j in range(2)]
        return sea, cells, moves, steady

    for i, r in ((0, 0), (1, ROWS - 8)):
        _, cells, moves, steady = tile_rows(r, 8)
        for k, tile in enumerate(cells + moves + steady):
            lat_packs[i, k] = tile

    def pack(i, carry):
        n = PACK
        r = pl.multiple_of(i * n, n)
        rows, padded = pl.ds(r, n), pl.ds(pl.multiple_of(r + 8, 8), n)
        sea, cells, moves, steady = tile_rows(r, n)
        mask[padded] = sea
        planes[12, padded] = steady[2]
        for ch in range(CHANNELS):
            field[ch, padded] = cells[ch]
        group, west_half = (iota(n, 1) >> 3) & 7, iota(n, 1) < 64
        first = lanes_of(cells[0], sent_cell)
        for ch in range(CHANNELS):
            if ch:
                first = jnp.where(group == 2 * ch, lanes_of(cells[ch], sent_cell), first)
            moved = lanes_of(moves[ch], sent_east if ch < 2 else sent_cell)
            first = jnp.where(group == 2 * ch + 1, moved * reflected(n) if ch < 2 else moved, first)
        second = lanes_of(steady[0], swapped_east)
        for k in range(1, 5):
            moved = lanes_of(steady[k], swapped_east if k == 3 else swapped_cell)
            second = jnp.where(group == k, moved, second)
        packs[0, rows] = jnp.where(west_half, second, first)
        packs[1, rows] = jnp.where(west_half, first, second)
        return carry

    lax.fori_loop(0, ROWS // PACK, pack, 0)

    def remote(src, dst, send, recv, to_lon, to_lat):
        return pltpu.make_async_remote_copy(
            src_ref=src,
            dst_ref=dst,
            send_sem=send,
            recv_sem=recv,
            device_id={"lon": to_lon, "lat": to_lat},
            device_id_type=MESH,
        )

    to_left = remote(packs.at[0], edges.at[1, pl.ds(8, ROWS)], lon_send.at[0], lon_recv.at[1], left, lat)
    to_right = remote(packs.at[1], edges.at[0, pl.ds(8, ROWS)], lon_send.at[1], lon_recv.at[0], right, lat)
    corner_row = pl.multiple_of(jnp.where(top, ROWS + 8, 0), 8)
    top_int = top.astype(jnp.int32)
    corner_ul = remote(
        packs.at[0, pl.ds(ROWS - 8, 8)],
        edges.at[1 - top_int, pl.ds(corner_row, 8)],
        corner_send.at[0],
        corner_recv.at[1 + top_int],
        up_left,
        up,
    )
    corner_ur = remote(
        packs.at[1, pl.ds(ROWS - 8, 8)],
        edges.at[top_int, pl.ds(corner_row, 8)],
        corner_send.at[1],
        corner_recv.at[3 * top_int],
        up_right,
        up,
    )
    corner_dl = remote(
        packs.at[0, pl.ds(0, 8)],
        edges.at[1, pl.ds(ROWS + 8, 8)],
        corner_send.at[2],
        corner_recv.at[3],
        left,
        down,
    )
    corner_dr = remote(
        packs.at[1, pl.ds(0, 8)],
        edges.at[0, pl.ds(ROWS + 8, 8)],
        corner_send.at[3],
        corner_recv.at[2],
        right,
        down,
    )
    to_up = remote(
        lat_packs.at[1], lat_edges.at[top_int], lat_send.at[0], lat_recv.at[top_int], up_lon, up
    )
    to_down = remote(lat_packs.at[0], lat_edges.at[1], lat_send.at[1], lat_recv.at[1], lon, down)

    pl.semaphore_wait(
        barrier,
        5
        - self_left.astype(jnp.int32)
        - self_right.astype(jnp.int32)
        + 3 * jnp.logical_not(bottom).astype(jnp.int32),
    )

    @pl.when(jnp.logical_not(self_left))
    def _():
        corner_ul.start()

    @pl.when(jnp.logical_not(self_right))
    def _():
        corner_ur.start()

    to_up.start()

    @pl.when(jnp.logical_not(bottom))
    def _():
        corner_dl.start()
        corner_dr.start()
        to_down.start()

    to_left.start()
    to_right.start()

    @pl.when(self_left)
    def _():
        edges[0, pl.ds(ROWS + 8, 8)] = packs[0, pl.ds(ROWS - 8, 8)]

    @pl.when(self_right)
    def _():
        edges[1, pl.ds(ROWS + 8, 8)] = packs[1, pl.ds(ROWS - 8, 8)]

    def prepare(i, carry):
        n = 64
        r = pl.multiple_of(i * n, n)
        rows, padded = pl.ds(r, n), pl.ds(pl.multiple_of(r + 8, 8), n)
        sea = mask[padded]
        open_east = sea * pltpu.roll(sea, LANES - 1, 1)
        open_north = sea * mask[pl.ds(r + 9, n)]
        regimes = [in_regime[j, rows].astype(F32) for j in range(2)]
        moves = [in_transport[j // 2, j % 2, rows] for j in range(4)]
        steady = [in_diffusion[j, rows] for j in range(2)] + [planes[12, padded]] + regimes
        for level in range(2):
            for way, opened in ((0, open_east), (1, open_north)):
                found = face_coefficients(moves[2 * way + level], steady[way], regimes[way], opened)
                for j in range(3):
                    planes[6 * level + 3 * way + j, padded] = found[j]
        cell, raw = own_strips([field[ch, padded] for ch in range(CHANNELS)], moves, steady)
        lon_field[0, pl.ds(pl.multiple_of(r + 16, 8), n)] = cell
        for a, strip in enumerate(raw):
            lon_raw[a, padded] = strip
        return carry

    lax.fori_loop(0, 4, prepare, 0)

    for ch in range(CHANNELS):
        lat_field[ch, pl.ds(16, 16)] = field[ch, pl.ds(8, 16)]
        lat_field[ch, pl.ds(32, 16)] = field[ch, pl.ds(ROWS - 8, 16)]
    for i in range(13):
        lat_planes[i, pl.ds(16, 16)] = planes[i, pl.ds(8, 16)]
        lat_planes[i, pl.ds(32, 16)] = planes[i, pl.ds(ROWS - 8, 16)]
    lat_mask[pl.ds(16, 16)] = mask[pl.ds(8, 16)]
    lat_mask[pl.ds(32, 16)] = mask[pl.ds(ROWS - 8, 16)]

    before = (lane - 2) & (LANES - 1)
    inner = 6 + ((lane + 2) & 3)
    patch_column = jnp.where(before < 64, inner, LANES - 1 - inner)

    def patch_lanes(n):
        return ((iota(n, 1) + 2) & 15) < 4

    def patch_of(channels):
        n = channels[0].shape[0]
        channel = (((iota(n, 1) - 2) & (LANES - 1)) >> 4) & 3
        got = [lanes_of(a, patch_column) for a in channels]
        result = got[0]
        for ch in range(1, CHANNELS):
            result = jnp.where(channel == ch, got[ch], result)
        return result

    def interior(step, carry):
        def run(source, target, kept, k):
            def chunk(i, c):
                start = pl.multiple_of(i * INNER + 8, 8)
                results = stage(source, target, kept, planes, flux, start, INNER, CHANNELS, 2)
                patches[k, pl.ds(start, INNER)] = patch_of(results)
                return c

            lax.fori_loop(0, ROWS // INNER, chunk, 0)

        run(field, guess, None, 2 * step)
        run(guess, field, field, 2 * step + 1)
        return carry

    lax.fori_loop(0, STEPS, interior, 0)

    remote(lat_edges.at[1], lat_edges.at[1], lat_send.at[0], lat_recv.at[1], lon, lat).wait_recv()

    @pl.when(jnp.logical_not(bottom))
    def _():
        remote(lat_edges.at[0], lat_edges.at[0], lat_send.at[0], lat_recv.at[0], lon, lat).wait_recv()

    row_cell, row_north = 7 - row8, jnp.maximum(6 - row8, 0)
    below = [lat_edges[0, k] for k in range(SENT)]
    norths = (6, 7, 9, 12)

    @pl.when(jnp.logical_not(top))
    def _():
        for k in range(SENT):
            lat_up[k] = lat_edges[1, k]

    @pl.when(top)
    def _():
        lane_cell, lane_east = LANES - 1 - lane, jnp.maximum(LANES - 2 - lane, 0)
        for k in range(SENT):
            turned = lanes(lat_edges[1, k], lane_east if k in (4, 5, 8, 11) else lane_cell)
            if k in (4, 5, 6, 7):
                turned = -turned
            lat_up[k] = sublanes(turned, row_north if k in norths else row_cell)
            if k in norths:
                lat_up[SENT + norths.index(k)] = sublanes(turned, row_cell)

    upper = [lat_up[k] for k in range(SENT)]
    lat_mask[pl.ds(8, 8)] = jnp.where(below[10] > 0.0, 1.0, 0.0)
    lat_mask[pl.ds(48, 8)] = jnp.where(upper[10] > 0.0, 1.0, 0.0)
    for ch in range(CHANNELS):
        lat_field[ch, pl.ds(8, 8)] = below[ch]
        lat_field[ch, pl.ds(48, 8)] = upper[ch]
    lat_planes[12, pl.ds(8, 8)] = below[10]
    lat_planes[12, pl.ds(48, 8)] = upper[10]
    highest = [lat_packs[1, k] for k in range(SENT)]
    for at, tiles in ((8, below), (40, highest), (48, upper)):
        sea = lat_mask[pl.ds(at, 8)]
        opened = (sea * pltpu.roll(sea, LANES - 1, 1), sea * lat_mask[pl.ds(at + 1, 8)])
        for level in range(2):
            for way in range(2):
                found = face_coefficients(
                    tiles[4 + 2 * way + level], tiles[8 + way], tiles[11 + way], opened[way]
                )
                for j in range(3):
                    lat_planes[6 * level + 3 * way + j, pl.ds(at, 8)] = found[j]

    @pl.when(jnp.logical_not(top))
    def _():
        for level in range(2):
            for j in range(3):
                lat_second[3 * level + j] = lat_planes[6 * level + 3 + j, pl.ds(47, 8)]

    @pl.when(top)
    def _():
        opened = lat_mask[pl.ds(47, 8)] * lat_mask[pl.ds(48, 8)]
        for level in range(2):
            found = face_coefficients(lat_up[13 + level], lat_up[15], lat_up[16], opened)
            for j in range(3):
                lat_second[3 * level + j] = found[j]

    lat_pair, lon_pair = (lat_field, lat_guess), (lon_field, lon_guess)
    for k in range(2 * STEPS):
        results = stage(
            lat_pair[k % 2],
            lat_pair[(k + 1) % 2],
            lat_field if k % 2 else None,
            lat_planes,
            lat_flux,
            8,
            48,
            CHANNELS,
            2,
            fold=(lat_second, 48),
        )
        if k < 2 * STEPS - 1:
            for at, to in ((0, 0), (32, ROWS)):
                patches[k, pl.ds(to, 16)] = patch_of([r[at : at + 16] for r in results])
    for ch in range(CHANNELS):
        field[ch, pl.ds(8, 8)] = lat_field[ch, pl.ds(16, 8)]
        field[ch, pl.ds(ROWS, 8)] = lat_field[ch, pl.ds(40, 8)]

    @pl.when(jnp.logical_not(bottom))
    def _():
        for side in range(2):
            remote(
                edges.at[side, pl.ds(0, 8)],
                edges.at[side, pl.ds(0, 8)],
                corner_send.at[0],
                corner_recv.at[side],
                lon,
                lat,
            ).wait_recv()

    @pl.when(jnp.logical_not(self_left))
    def _():
        remote(
            edges.at[0, pl.ds(ROWS + 8, 8)],
            edges.at[0, pl.ds(ROWS + 8, 8)],
            corner_send.at[0],
            corner_recv.at[2],
            lon,
            lat,
        ).wait_recv()

    @pl.when(jnp.logical_not(self_right))
    def _():
        remote(
            edges.at[1, pl.ds(ROWS + 8, 8)],
            edges.at[1, pl.ds(ROWS + 8, 8)],
            corner_send.at[0],
            corner_recv.at[3],
            lon,
            lat,
        ).wait_recv()

    for side in range(2):
        remote(
            edges.at[side, pl.ds(8, ROWS)],
            edges.at[side, pl.ds(8, ROWS)],
            lon_send.at[0],
            lon_recv.at[side],
            lon,
            lat,
        ).wait_recv()

    half = lane & 64
    far_index = [half + 16 * (j + level_lane) + 8 + place for j in (0, 2)]
    far_index += [(64 - half) + 8 * j + place for j in range(5)]

    def far_strips(west_edge, east_edge):
        west_half = iota(west_edge.shape[0], 1) < 64
        first = jnp.where(west_half, west_edge, east_edge)
        second = jnp.where(west_half, east_edge, west_edge)
        return first, [lanes_of(first if a < 2 else second, far_index[a]) for a in range(7)]

    def own_lanes(n, a):
        spot = iota(n, 1)
        if a in (0, 2, 5):
            return (spot & 15) >= jnp.where(spot < 64, 8, 7)
        return (spot & 15) >= 8

    cell, raw = own_strips(below[:4], below[4:8], below[8:])
    lon_field[0, pl.ds(8, 8)] = cell
    for a, strip in enumerate(raw):
        lon_raw[a, pl.ds(0, 8)] = strip

    @pl.when(jnp.logical_not(top))
    def _():
        cell, raw = own_strips(upper[:4], upper[4:8], upper[8:])
        lon_field[0, pl.ds(ROWS + 16, 8)] = cell
        for a, strip in enumerate(raw):
            lon_raw[a, pl.ds(ROWS + 8, 8)] = strip

    @pl.when(top)
    def _():
        across = [lat_edges[1, k] for k in range(SENT)]
        cell, raw = own_strips(across[:4], across[4:8], across[8:])
        far_cell, far_raw = far_strips(edges[1, pl.ds(ROWS + 8, 8)], edges[0, pl.ds(ROWS + 8, 8)])
        cell = jnp.where(own_lanes(8, 1), cell, far_cell)
        lon_field[0, pl.ds(ROWS + 16, 8)] = sublanes(pltpu.roll(cell, 64, 1), row_cell)
        for a in range(8):
            strip = raw[a] if a == 7 else jnp.where(own_lanes(8, a), raw[a], far_raw[a])
            turned = pltpu.roll(strip, 64, 1)
            if a == 1:
                turned = -turned
            lon_raw[a, pl.ds(ROWS + 8, 8)] = sublanes(turned, row_north if a in (1, 3, 6) else row_cell)
            if a in (1, 3, 6):
                lon_second[(1, 3, 6).index(a)] = sublanes(turned, row_cell)

    def join(i, carry):
        n = JOIN
        r = pl.multiple_of(i * n, 8)
        rows, padded = pl.ds(r, n), pl.ds(pl.multiple_of(r + 8, 8), n)
        whole = jnp.logical_and(iota(n, 0) + r >= ROWS + 8, top)
        whole_next = jnp.logical_and(iota(n, 0) + r >= ROWS + 7, top)
        west_edge, east_edge = edges[0, rows], edges[1, rows]
        first, far = far_strips(west_edge, east_edge)
        lon_field[0, padded] = jnp.where(
            jnp.logical_or(own_lanes(n, 1), whole), lon_field[0, padded], first
        )
        speed_east, speed_north, east_mix, north_mix, volume, east_rule, north_rule = [
            jnp.where(jnp.logical_or(own_lanes(n, a), whole), lon_raw[a, rows], far[a]) for a in range(7)
        ]
        lon_planes[6, padded] = volume
        ahead = pl.ds(r + 1, n)
        next_row = jnp.where(iota(n, 1) < 64, edges[1, ahead], edges[0, ahead])
        next_volume = jnp.where(
            jnp.logical_or(own_lanes(n, 4), whole_next),
            lon_raw[4, ahead],
            lanes_of(next_row, far_index[4]),
        )
        sea = jnp.where(volume > 0.0, 1.0, 0.0)
        sea_north = jnp.where(next_volume > 0.0, 1.0, 0.0)
        beyond_slot = jnp.where(lon_raw[7, rows] > 0.0, 1.0, 0.0)
        sea_east = jnp.where((iota(n, 1) & 15) == 15, beyond_slot, pltpu.roll(sea, LANES - 1, 1))
        found = face_coefficients(speed_east, east_mix, east_rule, sea * sea_east)
        found += face_coefficients(speed_north, north_mix, north_rule, sea * sea_north)
        for j in range(6):
            lon_planes[j, padded] = found[j]
        return carry

    lax.fori_loop(0, (ROWS + 16) // JOIN, join, 0)

    @pl.when(jnp.logical_not(top))
    def _():
        for j in range(3):
            lon_second[j] = lon_planes[3 + j, pl.ds(ROWS + 15, 8)]

    @pl.when(top)
    def _():
        seas = [jnp.where(lon_planes[6, pl.ds(ROWS + 15 + i, 8)] > 0.0, 1.0, 0.0) for i in range(2)]
        found = face_coefficients(*[lon_second[j] for j in range(3)], seas[0] * seas[1])
        for j in range(3):
            lon_second[j] = found[j]

    for k in range(2 * STEPS):
        last = k == 2 * STEPS - 1

        def patch(result):
            return jnp.where(patch_lanes(ROWS + 16), patches[k, pl.ds(0, ROWS + 16)], result)

        stage(
            lon_pair[k % 2],
            lon_pair[(k + 1) % 2],
            lon_field if k % 2 else None,
            lon_planes,
            lon_flux,
            8,
            ROWS + 16,
            1,
            1,
            fold=(lon_second, ROWS + 16),
            patch=None if last else patch,
        )

    def finish(i, carry):
        n = 128
        r = pl.multiple_of(i * n, n)
        rows, padded = pl.ds(r, n), pl.ds(pl.multiple_of(r + 8, 8), n)
        edge = lon_field[0, pl.ds(pl.multiple_of(r + 16, 8), n)]
        wide = iota(n, 1)
        kept = jnp.logical_and(wide >= 8, wide < LANES - 8)
        for ch in range(CHANNELS):
            index = 16 * ch + 8 + jnp.where(west_side, place, 64 + 7 - place)
            out[ch // 2, ch % 2, rows] = jnp.where(kept, field[ch, padded], lanes_of(edge, index))
        return carry

    lax.fori_loop(0, 2, finish, 0)

    to_left.wait_send()
    to_right.wait_send()
    to_up.wait_send()

    @pl.when(jnp.logical_not(self_left))
    def _():
        corner_ul.wait_send()

    @pl.when(jnp.logical_not(self_right))
    def _():
        corner_ur.wait_send()

    @pl.when(jnp.logical_not(bottom))
    def _():
        corner_dl.wait_send()
        corner_dr.wait_send()
        to_down.wait_send()


def solution(mesh):
    lon_count, lat_count = mesh.shape["lon"], mesh.shape["lat"]
    placed = (
        P(None, None, "lat", "lon"),
        P(None, None, "lat", "lon"),
        P(None, "lat", "lon"),
        P("lat", "lon"),
        P("lat", "lon"),
        P(None, "lat", "lon"),
    )

    def local(*arrays):
        shapes = [a.shape for a in arrays]
        types = [a.dtype for a in arrays]
        tall, wide = ROWS + 16, ROWS + 32

        def vmem(*shape):
            return pltpu.VMEM(shape, F32)

        return pl.pallas_call(
            functools.partial(kernel, lon_count, lat_count),
            out_shape=pltpu.VMEM(shapes[0], F32),
            in_specs=[pl.BlockSpec(memory_space=pl.ANY)] * 6,
            out_specs=pl.BlockSpec(memory_space=pltpu.VMEM),
            scratch_shapes=[
                *[pltpu.VMEM(s, t) for s, t in zip(shapes, types)],
                vmem(tall, LANES),
                vmem(CHANNELS, tall, LANES),
                vmem(CHANNELS, tall, LANES),
                vmem(13, tall, LANES),
                vmem(CHANNELS, tall, LANES),
                vmem(2, ROWS, LANES),
                vmem(2, tall + 8, LANES),
                vmem(2, SENT, 8, LANES),
                vmem(2, SENT, 8, LANES),
                vmem(64, LANES),
                vmem(CHANNELS, 64, LANES),
                vmem(CHANNELS, 64, LANES),
                vmem(13, 64, LANES),
                vmem(CHANNELS, 64, LANES),
                vmem(SENT + 4, 8, LANES),
                vmem(6, 8, LANES),
                vmem(8, tall + 8, LANES),
                vmem(1, wide, LANES),
                vmem(1, wide, LANES),
                vmem(7, wide, LANES),
                vmem(1, wide, LANES),
                vmem(3, 8, LANES),
                vmem(2 * STEPS, tall, LANES),
                pltpu.SemaphoreType.DMA((6,)),
                pltpu.SemaphoreType.DMA((2,)),
                pltpu.SemaphoreType.DMA((2,)),
                pltpu.SemaphoreType.DMA((2,)),
                pltpu.SemaphoreType.DMA((2,)),
                pltpu.SemaphoreType.DMA((4,)),
                pltpu.SemaphoreType.DMA((4,)),
            ],
            compiler_params=pltpu.CompilerParams(
                collective_id=0, has_side_effects=True, vmem_limit_bytes=64900 * 1024
            ),
        )(*arrays)

    return jax.shard_map(
        local, mesh=mesh, in_specs=placed, out_specs=P(None, None, "lat", "lon"), check_vma=False
    )
```

```python
import functools

import jax
import jax.numpy as jnp
from jax import lax
from jax.experimental import pallas as pl
from jax.experimental.pallas import tpu as pltpu
from jax.sharding import PartitionSpec as P

STEPS = 2
MESH = pl.DeviceIdType.MESH
HALO = 8
ROWS = 256
LANES = 128
CHANNELS = 4
F32 = jnp.float32
INNER = 256
PREP = 64
JOIN = 136
GROUP = 72

SENT = 13


def iota(rows, axis):
    return lax.broadcasted_iota(jnp.int32, (rows, LANES), axis)


def lanes(tile, index):
    return jnp.take_along_axis(tile, index, axis=1, mode="promise_in_bounds")


def sublanes(tile, index):
    return jnp.take_along_axis(tile, index, axis=0, mode="promise_in_bounds")


def lanes_of(rows, index):
    tiles = [lanes(rows[8 * i : 8 * i + 8], index) for i in range(rows.shape[0] // 8)]
    return tiles[0] if len(tiles) == 1 else jnp.concatenate(tiles, axis=0)


def face_flux(cell, gap, gap_behind, gap_beyond, a, b, c):
    other = jnp.where(a > 0.0, gap_behind, gap_beyond)
    slope = jnp.maximum(jnp.minimum(gap, 0.0), jnp.minimum(other, jnp.maximum(gap, 0.0)))
    return a * cell + b * gap + c * slope


def face_coefficients(velocity, conduct, regime, opened):
    a = opened * velocity
    share = jnp.where(regime == 1.0, 0.5, jnp.where(velocity > 0.0, 0.0, 1.0))
    b = a * share - opened * conduct
    c = jnp.where(regime == 2.0, 0.5 * jnp.abs(a), 0.0)
    return a, b, c


def stage(source, target, kept, planes, north_flux, start, count, channels, levels, fold=None, patch=None):
    rows = pl.ds(start, count)
    volume = planes[6 * levels, rows]
    results = []
    for ch in range(channels):
        level = 6 * (ch % levels)

        def plane(i):
            return planes[level + i, rows]

        cell = source[ch, rows]
        behind = source[ch, pl.ds(start - 1, count)]
        ahead = source[ch, pl.ds(start + 1, count)]
        beyond = source[ch, pl.ds(start + 2, count)]
        north = face_flux(
            cell, ahead - cell, cell - behind, beyond - ahead, plane(3), plane(4), plane(5)
        )
        north_flux[ch, rows] = north
        if fold is not None:
            second, row = fold
            at = [source[ch, pl.ds(row + i, 8)] for i in (-2, -1, 0, 1)]
            theirs = face_flux(
                at[1],
                at[2] - at[1],
                at[1] - at[0],
                at[3] - at[2],
                *[second[3 * (ch % levels) + i] for i in range(3)],
            )
            north_flux[ch, pl.ds(row - 1, 1)] = theirs[0:1]
        east1 = pltpu.roll(cell, LANES - 1, 1)
        east2 = pltpu.roll(cell, LANES - 2, 1)
        west1 = pltpu.roll(cell, 1, 1)
        east = face_flux(
            cell,
            east1 - cell,
            cell - west1,
            east2 - east1,
            plane(0),
            plane(1),
            plane(2),
        )
        west = pltpu.roll(east, 1, 1)
        south = north_flux[ch, pl.ds(start - 1, count)]
        result = volume * ((west - east) + (south - north))
        if kept is None:
            result = cell + result
        else:
            result = 0.5 * ((kept[ch, rows] + cell) + result)
        if patch is not None:
            result = patch(result)
        target[ch, rows] = result
        results.append(result)
    return results


def unit(source, target, kept, planes, north_flux, ch, levels, start, count, fold, patch, results):
    rows, level = pl.ds(start, count), 6 * (ch % levels)
    cell = source[ch, rows]
    east1 = pltpu.roll(cell, LANES - 1, 1)
    west1 = pltpu.roll(cell, 1, 1)
    east2 = pltpu.roll(cell, LANES - 2, 1)
    yield
    behind = source[ch, pl.ds(start - 1, count)]
    ahead = source[ch, pl.ds(start + 1, count)]
    beyond = source[ch, pl.ds(start + 2, count)]
    north = face_flux(
        cell, ahead - cell, cell - behind, beyond - ahead, *[planes[level + i, rows] for i in (3, 4, 5)]
    )
    north_flux[ch, rows] = north
    if fold is not None and start <= fold[1] - 1 < start + count:
        second, row = fold
        at = [source[ch, pl.ds(row + i, 8)] for i in (-2, -1, 0, 1)]
        theirs = face_flux(
            at[1],
            at[2] - at[1],
            at[1] - at[0],
            at[3] - at[2],
            *[second[3 * (ch % levels) + i] for i in range(3)],
        )
        north_flux[ch, pl.ds(row - 1, 1)] = theirs[0:1]
    yield
    east = face_flux(
        cell, east1 - cell, cell - west1, east2 - east1, *[planes[level + i, rows] for i in range(3)]
    )
    west = pltpu.roll(east, 1, 1)
    yield
    south = north_flux[ch, pl.ds(start - 1, count)]
    result = planes[6 * levels, rows] * ((west - east) + (south - north))
    if kept is None:
        result = cell + result
    else:
        result = 0.5 * ((kept[ch, rows] + cell) + result)
    if patch is not None:
        result = patch(result, rows)
    target[ch, rows] = result
    results.append(result)


def pipeline(units):
    for turn in range(len(units) + 3):
        for phase in range(4):
            if 0 <= turn - phase < len(units):
                next(units[turn - phase], None)


def kernel(
    lon_count,
    lat_count,
    tracer,
    transport,
    diffusion,
    inverse_volume,
    sea_mask,
    regime,
    out,
    in_tracer,
    in_transport,
    in_diffusion,
    in_volume,
    in_mask,
    in_regime,
    mask,
    field,
    guess,
    planes,
    flux,
    packs,
    edges,
    lat_packs,
    lat_edges,
    lat_mask,
    lat_field,
    lat_guess,
    lat_planes,
    lat_flux,
    lat_second,
    lon_raw,
    lon_field,
    lon_guess,
    lon_planes,
    lon_flux,
    lon_second,
    patches,
    load_sem,
    lat_send,
    lat_recv,
    lon_send,
    lon_recv,
    corner_send,
    corner_recv,
):
    lon = lax.axis_index("lon")
    lat = lax.axis_index("lat")
    top = lat == lat_count - 1
    bottom = lat == 0
    left = lax.rem(lon + lon_count - 1, lon_count)
    right = lax.rem(lon + 1, lon_count)
    up = jnp.where(top, lat, lat + 1)
    up_lon = jnp.where(top, lon_count - 1 - lon, lon)
    up_left = jnp.where(top, lax.rem(lon_count - lon, lon_count), left)
    up_right = jnp.where(top, lax.rem(2 * lon_count - 2 - lon, lon_count), right)
    self_left = jnp.logical_and(top, up_left == lon)
    self_right = jnp.logical_and(top, up_right == lon)
    down = jnp.where(bottom, lat, lat - 1)

    barrier = pltpu.get_barrier_semaphore()

    def greet(to_lon, to_lat):
        pl.semaphore_signal(
            barrier, inc=1, device_id={"lon": to_lon, "lat": to_lat}, device_id_type=MESH
        )

    @pl.when(jnp.logical_not(self_left))
    def _():
        greet(up_left, up)

    @pl.when(jnp.logical_not(self_right))
    def _():
        greet(up_right, up)

    @pl.when(jnp.logical_not(bottom))
    def _():
        greet(left, down)
        greet(right, down)
        greet(lon, down)

    greet(up_lon, up)
    greet(left, lat)
    greet(right, lat)

    arrays = (tracer, transport, diffusion, inverse_volume, sea_mask, regime)
    held = (in_tracer, in_transport, in_diffusion, in_volume, in_mask, in_regime)
    loads = [pltpu.make_async_copy(a, h, load_sem.at[i]) for i, (a, h) in enumerate(zip(arrays, held))]
    for load in loads:
        load.start()

    pad = jnp.zeros((8, LANES), F32)
    for ref in (field, guess, flux, planes):
        for i in range(ref.shape[0]):
            ref[i, pl.ds(0, 8)] = pad
            ref[i, pl.ds(8 + ROWS, 8)] = pad
    mask[pl.ds(ROWS + 8, 8)] = pad
    for ref in (lat_field, lat_guess, lat_flux):
        for i in range(ref.shape[0]):
            ref[i, pl.ds(0, 8)] = pad
            ref[i, pl.ds(56, 8)] = pad
    for ref in (lon_field, lon_guess, lon_flux):
        ref[0, pl.ds(0, 8)] = pad
        ref[0, pl.ds(24 + ROWS, 8)] = pad
    lat_mask[pl.ds(56, 8)] = pad
    lon_raw[4, pl.ds(ROWS + 16, 8)] = pad
    for i in range(2):
        edges[i, pl.ds(ROWS + 16, 8)] = pad

    @pl.when(bottom)
    def _():
        lat_edges[0] = jnp.zeros(lat_edges.shape[1:], F32)
        for i in range(2):
            edges[i, pl.ds(0, 8)] = pad

    for load in loads:
        load.wait()

    lane, row8 = iota(8, 1), iota(8, 0)
    place, west_side = lane & 7, lane < 64
    own_cell = jnp.where(west_side, place, LANES - 1 - place)
    own_east = jnp.where(
        west_side, place, jnp.where((lane & 15) >= 8, LANES - 2 - place, LANES - 1)
    )
    level_lane = (lane >> 4) & 1
    sent_cell = jnp.where(west_side, LANES - 8 + place, 7 - place)
    sent_east = jnp.where(west_side, LANES - 8 + place, jnp.maximum(6 - place, 0))
    swapped_cell = jnp.where(west_side, 7 - place, LANES - 8 + place)
    swapped_east = jnp.where(west_side, jnp.maximum(6 - place, 0), LANES - 8 + place)

    def reflected(n):
        return jnp.where(iota(n, 1) < 64, 1.0, -1.0)

    def own_strips(cells, moves, steady):
        n = cells[0].shape[0]
        channel, odd = (iota(n, 1) >> 4) & 3, ((iota(n, 1) >> 4) & 1) == 1
        got = [lanes_of(a, own_cell) for a in cells]
        cell = got[0]
        for ch in range(1, CHANNELS):
            cell = jnp.where(channel == ch, got[ch], cell)
        speed_east = [lanes_of(a, own_east) for a in moves[:2]]
        speed_north = [lanes_of(a, own_cell) for a in moves[2:]]
        return cell, [
            jnp.where(odd, speed_east[1], speed_east[0]) * reflected(n),
            jnp.where(odd, speed_north[1], speed_north[0]),
            lanes_of(steady[0], own_east),
            lanes_of(steady[1], own_cell),
            lanes_of(steady[2], own_cell),
            lanes_of(steady[3], own_east),
            lanes_of(steady[4], own_cell),
            lanes_of(steady[2], own_next),
        ]

    own_next = jnp.where(west_side, place + 1, LANES - 2 - place)

    def tile_rows(r, n):
        rows = pl.ds(r, n)
        sea = in_mask[rows].astype(F32)
        cells = [in_tracer[ch // 2, ch % 2, rows] * sea for ch in range(CHANNELS)]
        moves = [in_transport[j // 2, j % 2, rows] for j in range(4)]
        steady = [in_diffusion[j, rows] for j in range(2)]
        steady += [in_volume[rows] * sea]
        steady += [in_regime[j, rows].astype(F32) for j in range(2)]
        return sea, cells, moves, steady

    for i, r in ((0, 0), (1, ROWS - 8)):
        _, cells, moves, steady = tile_rows(r, 8)
        for k, tile in enumerate(cells + moves + steady):
            lat_packs[i, k] = tile

    def pack(r, n):
        rows, padded = pl.ds(r, n), pl.ds(r + 8, n)
        sea, cells, moves, steady = tile_rows(r, n)
        mask[padded] = sea
        planes[12, padded] = steady[2]
        for ch in range(CHANNELS):
            field[ch, padded] = cells[ch]
        group, west_half = (iota(n, 1) >> 3) & 7, iota(n, 1) < 64
        first = lanes_of(cells[0], sent_cell)
        for ch in range(CHANNELS):
            if ch:
                first = jnp.where(group == 2 * ch, lanes_of(cells[ch], sent_cell), first)
            moved = lanes_of(moves[ch], sent_east if ch < 2 else sent_cell)
            first = jnp.where(group == 2 * ch + 1, moved * reflected(n) if ch < 2 else moved, first)
        second = lanes_of(steady[0], swapped_east)
        for k in range(1, 5):
            moved = lanes_of(steady[k], swapped_east if k == 3 else swapped_cell)
            second = jnp.where(group == k, moved, second)
        packs[0, rows] = jnp.where(west_half, second, first)
        packs[1, rows] = jnp.where(west_half, first, second)

    pack(0, ROWS)

    def remote(src, dst, send, recv, to_lon, to_lat):
        return pltpu.make_async_remote_copy(
            src_ref=src,
            dst_ref=dst,
            send_sem=send,
            recv_sem=recv,
            device_id={"lon": to_lon, "lat": to_lat},
            device_id_type=MESH,
        )

    to_left = remote(packs.at[0], edges.at[1, pl.ds(8, ROWS)], lon_send.at[0], lon_recv.at[1], left, lat)
    to_right = remote(packs.at[1], edges.at[0, pl.ds(8, ROWS)], lon_send.at[1], lon_recv.at[0], right, lat)
    corner_row = pl.multiple_of(jnp.where(top, ROWS + 8, 0), 8)
    top_int = top.astype(jnp.int32)
    corner_ul = remote(
        packs.at[0, pl.ds(ROWS - 8, 8)],
        edges.at[1 - top_int, pl.ds(corner_row, 8)],
        corner_send.at[0],
        corner_recv.at[1 + top_int],
        up_left,
        up,
    )
    corner_ur = remote(
        packs.at[1, pl.ds(ROWS - 8, 8)],
        edges.at[top_int, pl.ds(corner_row, 8)],
        corner_send.at[1],
        corner_recv.at[3 * top_int],
        up_right,
        up,
    )
    corner_dl = remote(
        packs.at[0, pl.ds(0, 8)],
        edges.at[1, pl.ds(ROWS + 8, 8)],
        corner_send.at[2],
        corner_recv.at[3],
        left,
        down,
    )
    corner_dr = remote(
        packs.at[1, pl.ds(0, 8)],
        edges.at[0, pl.ds(ROWS + 8, 8)],
        corner_send.at[3],
        corner_recv.at[2],
        right,
        down,
    )
    to_up = remote(
        lat_packs.at[1], lat_edges.at[top_int], lat_send.at[0], lat_recv.at[top_int], up_lon, up
    )
    to_down = remote(lat_packs.at[0], lat_edges.at[1], lat_send.at[1], lat_recv.at[1], lon, down)

    pl.semaphore_wait(
        barrier,
        5
        - self_left.astype(jnp.int32)
        - self_right.astype(jnp.int32)
        + 3 * jnp.logical_not(bottom).astype(jnp.int32),
    )

    @pl.when(jnp.logical_not(self_left))
    def _():
        corner_ul.start()

    @pl.when(jnp.logical_not(self_right))
    def _():
        corner_ur.start()

    to_up.start()

    @pl.when(jnp.logical_not(bottom))
    def _():
        corner_dl.start()
        corner_dr.start()
        to_down.start()

    to_left.start()
    to_right.start()

    @pl.when(self_left)
    def _():
        edges[0, pl.ds(ROWS + 8, 8)] = packs[0, pl.ds(ROWS - 8, 8)]

    @pl.when(self_right)
    def _():
        edges[1, pl.ds(ROWS + 8, 8)] = packs[1, pl.ds(ROWS - 8, 8)]

    def prepare(r, n):
        rows, padded = pl.ds(r, n), pl.ds(r + 8, n)
        sea = mask[padded]
        open_east = sea * pltpu.roll(sea, LANES - 1, 1)
        open_north = sea * mask[pl.ds(r + 9, n)]
        regimes = [in_regime[j, rows].astype(F32) for j in range(2)]
        moves = [in_transport[j // 2, j % 2, rows] for j in range(4)]
        steady = [in_diffusion[j, rows] for j in range(2)] + [planes[12, padded]] + regimes
        for level in range(2):
            for way, opened in ((0, open_east), (1, open_north)):
                found = face_coefficients(moves[2 * way + level], steady[way], regimes[way], opened)
                for j in range(3):
                    planes[6 * level + 3 * way + j, padded] = found[j]
        cell, raw = own_strips([field[ch, padded] for ch in range(CHANNELS)], moves, steady)
        lon_field[0, pl.ds(r + 16, n)] = cell
        for a, strip in enumerate(raw):
            lon_raw[a, padded] = strip

    for r in range(0, ROWS, PREP):
        prepare(r, PREP)

    for ch in range(CHANNELS):
        lat_field[ch, pl.ds(16, 16)] = field[ch, pl.ds(8, 16)]
        lat_field[ch, pl.ds(32, 16)] = field[ch, pl.ds(ROWS - 8, 16)]
    for i in range(13):
        lat_planes[i, pl.ds(16, 16)] = planes[i, pl.ds(8, 16)]
        lat_planes[i, pl.ds(32, 16)] = planes[i, pl.ds(ROWS - 8, 16)]
    lat_mask[pl.ds(16, 16)] = mask[pl.ds(8, 16)]
    lat_mask[pl.ds(32, 16)] = mask[pl.ds(ROWS - 8, 16)]

    before = (lane - 2) & (LANES - 1)
    inner = 6 + ((lane + 2) & 3)
    patch_column = jnp.where(before < 64, inner, LANES - 1 - inner)

    def patch_lanes(n):
        return ((iota(n, 1) + 2) & 15) < 4

    def patch_of(channels):
        n = channels[0].shape[0]
        channel = (((iota(n, 1) - 2) & (LANES - 1)) >> 4) & 3
        got = [lanes_of(a, patch_column) for a in channels]
        result = got[0]
        for ch in range(1, CHANNELS):
            result = jnp.where(channel == ch, got[ch], result)
        return result

    def interior(step, carry):
        def run(source, target, kept, k):
            def chunk(i, c):
                start = pl.multiple_of(i * INNER + 8, 8)
                results = stage(source, target, kept, planes, flux, start, INNER, CHANNELS, 2)
                patches[k, pl.ds(start, INNER)] = patch_of(results)
                return c

            lax.fori_loop(0, ROWS // INNER, chunk, 0)

        run(field, guess, None, 2 * step)
        run(guess, field, field, 2 * step + 1)
        return carry

    lax.fori_loop(0, STEPS, interior, 0)

    remote(lat_edges.at[1], lat_edges.at[1], lat_send.at[0], lat_recv.at[1], lon, lat).wait_recv()

    @pl.when(jnp.logical_not(bottom))
    def _():
        remote(lat_edges.at[0], lat_edges.at[0], lat_send.at[0], lat_recv.at[0], lon, lat).wait_recv()

    below = [lat_edges[0, k] for k in range(SENT)]
    across = [lat_edges[1, k] for k in range(SENT)]
    norths = (6, 7, 9, 12)
    row_cell = jnp.where(top, 7 - row8, row8)
    row_north = jnp.where(top, jnp.maximum(6 - row8, 0), row8)
    sign = jnp.where(top, -1.0, 1.0)
    lane_cell = jnp.where(top, LANES - 1 - lane, lane)
    lane_east = jnp.where(top, jnp.maximum(LANES - 2 - lane, 0), lane)
    upper, second_raw = [], []
    for k in range(SENT):
        turned = lanes(across[k], lane_east if k in (4, 5, 8, 11) else lane_cell)
        if k in (4, 5, 6, 7):
            turned = turned * sign
        upper.append(sublanes(turned, row_north if k in norths else row_cell))
        if k in norths:
            second_raw.append(sublanes(turned, row_cell))

    lat_mask[pl.ds(8, 8)] = jnp.where(below[10] > 0.0, 1.0, 0.0)
    lat_mask[pl.ds(48, 8)] = jnp.where(upper[10] > 0.0, 1.0, 0.0)
    for ch in range(CHANNELS):
        lat_field[ch, pl.ds(8, 8)] = below[ch]
        lat_field[ch, pl.ds(48, 8)] = upper[ch]
    lat_planes[12, pl.ds(8, 8)] = below[10]
    lat_planes[12, pl.ds(48, 8)] = upper[10]
    highest = [lat_packs[1, k] for k in range(SENT)]
    for at, tiles in ((8, below), (40, highest), (48, upper)):
        sea = lat_mask[pl.ds(at, 8)]
        opened = (sea * pltpu.roll(sea, LANES - 1, 1), sea * lat_mask[pl.ds(at + 1, 8)])
        for level in range(2):
            for way in range(2):
                found = face_coefficients(
                    tiles[4 + 2 * way + level], tiles[8 + way], tiles[11 + way], opened[way]
                )
                for j in range(3):
                    lat_planes[6 * level + 3 * way + j, pl.ds(at, 8)] = found[j]

    opened = lat_mask[pl.ds(47, 8)] * lat_mask[pl.ds(48, 8)]
    for level in range(2):
        found = face_coefficients(second_raw[level], second_raw[2], second_raw[3], opened)
        for j in range(3):
            lat_second[3 * level + j] = jnp.where(top, found[j], lat_planes[6 * level + 3 + j, pl.ds(47, 8)])

    lat_pair, lon_pair = (lat_field, lat_guess), (lon_field, lon_guess)

    def lat_units(k, results):
        return [
            unit(
                lat_pair[k % 2],
                lat_pair[(k + 1) % 2],
                lat_field if k % 2 else None,
                lat_planes,
                lat_flux,
                ch,
                2,
                start,
                count,
                (lat_second, 48),
                None,
                results,
            )
            for ch in range(CHANNELS)
            for start, count in (((8, 48),) if k < 2 * STEPS - 1 else ((8, 16), (32, 16)))
        ]

    def lon_units(k):
        def patch(result, rows):
            n = result.shape[0]
            return jnp.where(patch_lanes(n), patches[k, pl.ds(rows.start - 8, n)], result)

        return [
            unit(
                lon_pair[k % 2],
                lon_pair[(k + 1) % 2],
                lon_field if k % 2 else None,
                lon_planes,
                lon_flux,
                0,
                1,
                8 + r,
                min(GROUP, ROWS + 16 - r),
                (lon_second, ROWS + 16),
                None if k == 2 * STEPS - 1 else patch,
                [],
            )
            for r in range(0, ROWS + 16, GROUP)
        ]

    def lat_done(k, results):
        if k < 2 * STEPS - 1:
            for at, to in ((0, 0), (32, ROWS)):
                patches[k, pl.ds(to, 16)] = patch_of([r[at : at + 16] for r in results])
        else:
            for ch in range(CHANNELS):
                field[ch, pl.ds(8, 8)] = lat_field[ch, pl.ds(16, 8)]
                field[ch, pl.ds(ROWS, 8)] = lat_field[ch, pl.ds(40, 8)]

    for k in range(2 * STEPS):
        results = []
        pipeline(lat_units(k, results))
        lat_done(k, results)

    @pl.when(jnp.logical_not(bottom))
    def _():
        for side in range(2):
            remote(
                edges.at[side, pl.ds(0, 8)],
                edges.at[side, pl.ds(0, 8)],
                corner_send.at[0],
                corner_recv.at[side],
                lon,
                lat,
            ).wait_recv()

    @pl.when(jnp.logical_not(self_left))
    def _():
        remote(
            edges.at[0, pl.ds(ROWS + 8, 8)],
            edges.at[0, pl.ds(ROWS + 8, 8)],
            corner_send.at[0],
            corner_recv.at[2],
            lon,
            lat,
        ).wait_recv()

    @pl.when(jnp.logical_not(self_right))
    def _():
        remote(
            edges.at[1, pl.ds(ROWS + 8, 8)],
            edges.at[1, pl.ds(ROWS + 8, 8)],
            corner_send.at[0],
            corner_recv.at[3],
            lon,
            lat,
        ).wait_recv()

    for side in range(2):
        remote(
            edges.at[side, pl.ds(8, ROWS)],
            edges.at[side, pl.ds(8, ROWS)],
            lon_send.at[0],
            lon_recv.at[side],
            lon,
            lat,
        ).wait_recv()

    half = lane & 64
    far_index = [half + 16 * (j + level_lane) + 8 + place for j in (0, 2)]
    far_index += [(64 - half) + 8 * j + place for j in range(5)]

    def far_strips(west_edge, east_edge):
        west_half = iota(west_edge.shape[0], 1) < 64
        first = jnp.where(west_half, west_edge, east_edge)
        second = jnp.where(west_half, east_edge, west_edge)
        return first, [lanes_of(first if a < 2 else second, far_index[a]) for a in range(7)]

    def own_lanes(n, a):
        spot = iota(n, 1)
        if a in (0, 2, 5):
            return (spot & 15) >= jnp.where(spot < 64, 8, 7)
        return (spot & 15) >= 8

    cell, raw = own_strips(below[:4], below[4:8], below[8:])
    lon_field[0, pl.ds(8, 8)] = cell
    for a, strip in enumerate(raw):
        lon_raw[a, pl.ds(0, 8)] = strip

    cell, raw = own_strips(across[:4], across[4:8], across[8:])
    corners = [edges[side, pl.ds(ROWS + 8, 8)] for side in range(2)]
    far_cell, far_raw = far_strips(
        jnp.where(top, corners[1], corners[0]), jnp.where(top, corners[0], corners[1])
    )
    side_swap = jnp.where(top, lane ^ 64, lane)
    cell = lanes(jnp.where(own_lanes(8, 1), cell, far_cell), side_swap)
    lon_field[0, pl.ds(ROWS + 16, 8)] = sublanes(cell, row_cell)
    second_raw = []
    for a in range(8):
        strip = raw[a] if a == 7 else jnp.where(own_lanes(8, a), raw[a], far_raw[a])
        turned = lanes(strip, side_swap)
        if a == 1:
            turned = turned * sign
        lon_raw[a, pl.ds(ROWS + 8, 8)] = sublanes(turned, row_north if a in (1, 3, 6) else row_cell)
        if a in (1, 3, 6):
            second_raw.append(sublanes(turned, row_cell))

    def join(r, n):
        rows, padded = pl.ds(r, n), pl.ds(r + 8, n)
        whole = iota(n, 0) + r >= ROWS + 8
        whole_next = iota(n, 0) + r >= ROWS + 7
        west_edge, east_edge = edges[0, rows], edges[1, rows]
        first, far = far_strips(west_edge, east_edge)
        lon_field[0, padded] = jnp.where(
            jnp.logical_or(own_lanes(n, 1), whole), lon_field[0, padded], first
        )
        speed_east, speed_north, east_mix, north_mix, volume, east_rule, north_rule = [
            jnp.where(jnp.logical_or(own_lanes(n, a), whole), lon_raw[a, rows], far[a]) for a in range(7)
        ]
        lon_planes[6, padded] = volume
        ahead = pl.ds(r + 1, n)
        next_row = jnp.where(iota(n, 1) < 64, edges[1, ahead], edges[0, ahead])
        next_volume = jnp.where(
            jnp.logical_or(own_lanes(n, 4), whole_next),
            lon_raw[4, ahead],
            lanes_of(next_row, far_index[4]),
        )
        sea = jnp.where(volume > 0.0, 1.0, 0.0)
        sea_north = jnp.where(next_volume > 0.0, 1.0, 0.0)
        beyond_slot = jnp.where(lon_raw[7, rows] > 0.0, 1.0, 0.0)
        sea_east = jnp.where((iota(n, 1) & 15) == 15, beyond_slot, pltpu.roll(sea, LANES - 1, 1))
        found = face_coefficients(speed_east, east_mix, east_rule, sea * sea_east)
        found += face_coefficients(speed_north, north_mix, north_rule, sea * sea_north)
        for j in range(6):
            lon_planes[j, padded] = found[j]

    for r in range(0, ROWS + 16, JOIN):
        join(r, JOIN)

    seas = [jnp.where(lon_planes[6, pl.ds(ROWS + 15 + i, 8)] > 0.0, 1.0, 0.0) for i in range(2)]
    found = face_coefficients(*second_raw, seas[0] * seas[1])
    for j in range(3):
        lon_second[j] = jnp.where(top, found[j], lon_planes[3 + j, pl.ds(ROWS + 15, 8)])

    for k in range(2 * STEPS):
        pipeline(lon_units(k))

    def finish(r, n):
        rows, padded = pl.ds(r, n), pl.ds(r + 8, n)
        edge = lon_field[0, pl.ds(r + 16, n)]
        wide = iota(n, 1)
        kept = jnp.logical_and(wide >= 8, wide < LANES - 8)
        for ch in range(CHANNELS):
            index = 16 * ch + 8 + jnp.where(west_side, place, 64 + 7 - place)
            out[ch // 2, ch % 2, rows] = jnp.where(kept, field[ch, padded], lanes_of(edge, index))

    finish(0, ROWS)

    to_left.wait_send()
    to_right.wait_send()
    to_up.wait_send()

    @pl.when(jnp.logical_not(self_left))
    def _():
        corner_ul.wait_send()

    @pl.when(jnp.logical_not(self_right))
    def _():
        corner_ur.wait_send()

    @pl.when(jnp.logical_not(bottom))
    def _():
        corner_dl.wait_send()
        corner_dr.wait_send()
        to_down.wait_send()


def solution(mesh):
    lon_count, lat_count = mesh.shape["lon"], mesh.shape["lat"]
    placed = (
        P(None, None, "lat", "lon"),
        P(None, None, "lat", "lon"),
        P(None, "lat", "lon"),
        P("lat", "lon"),
        P("lat", "lon"),
        P(None, "lat", "lon"),
    )

    def local(*arrays):
        shapes = [a.shape for a in arrays]
        types = [a.dtype for a in arrays]
        tall, wide = ROWS + 16, ROWS + 32

        def vmem(*shape):
            return pltpu.VMEM(shape, F32)

        return pl.pallas_call(
            functools.partial(kernel, lon_count, lat_count),
            out_shape=pltpu.VMEM(shapes[0], F32),
            in_specs=[pl.BlockSpec(memory_space=pl.ANY)] * 6,
            out_specs=pl.BlockSpec(memory_space=pltpu.VMEM),
            scratch_shapes=[
                *[pltpu.VMEM(s, t) for s, t in zip(shapes, types)],
                vmem(tall, LANES),
                vmem(CHANNELS, tall, LANES),
                vmem(CHANNELS, tall, LANES),
                vmem(13, tall, LANES),
                vmem(CHANNELS, tall, LANES),
                vmem(2, ROWS, LANES),
                vmem(2, tall + 8, LANES),
                vmem(2, SENT, 8, LANES),
                vmem(2, SENT, 8, LANES),
                vmem(64, LANES),
                vmem(CHANNELS, 64, LANES),
                vmem(CHANNELS, 64, LANES),
                vmem(13, 64, LANES),
                vmem(CHANNELS, 64, LANES),
                vmem(6, 8, LANES),
                vmem(8, tall + 8, LANES),
                vmem(1, wide, LANES),
                vmem(1, wide, LANES),
                vmem(7, wide, LANES),
                vmem(1, wide, LANES),
                vmem(3, 8, LANES),
                vmem(2 * STEPS, tall, LANES),
                pltpu.SemaphoreType.DMA((6,)),
                pltpu.SemaphoreType.DMA((2,)),
                pltpu.SemaphoreType.DMA((2,)),
                pltpu.SemaphoreType.DMA((2,)),
                pltpu.SemaphoreType.DMA((2,)),
                pltpu.SemaphoreType.DMA((4,)),
                pltpu.SemaphoreType.DMA((4,)),
            ],
            compiler_params=pltpu.CompilerParams(
                collective_id=0, has_side_effects=True, vmem_limit_bytes=64900 * 1024
            ),
        )(*arrays)

    return jax.shard_map(
        local, mesh=mesh, in_specs=placed, out_specs=P(None, None, "lat", "lon"), check_vma=False
    )
```

```python
import functools

import jax
import jax.numpy as jnp
from jax import lax
from jax.experimental import pallas as pl
from jax.experimental.pallas import tpu as pltpu
from jax.sharding import PartitionSpec as P

STEPS = 2
MESH = pl.DeviceIdType.MESH
HALO = 8
ROWS = 256
LANES = 128
CHANNELS = 4
F32 = jnp.float32
INNER = 256
PREP = 64
GROUP = 72

SENT = 13


def iota(rows, axis):
    return lax.broadcasted_iota(jnp.int32, (rows, LANES), axis)


def lanes(tile, index):
    return jnp.take_along_axis(tile, index, axis=1, mode="promise_in_bounds")


def sublanes(tile, index):
    return jnp.take_along_axis(tile, index, axis=0, mode="promise_in_bounds")


def lanes_of(rows, index):
    tiles = [lanes(rows[8 * i : 8 * i + 8], index) for i in range(rows.shape[0] // 8)]
    return tiles[0] if len(tiles) == 1 else jnp.concatenate(tiles, axis=0)


def face_flux(cell, gap, gap_behind, gap_beyond, a, b, c):
    other = jnp.where(a > 0.0, gap_behind, gap_beyond)
    slope = jnp.maximum(jnp.minimum(gap, 0.0), jnp.minimum(other, jnp.maximum(gap, 0.0)))
    return a * cell + b * gap + c * slope


def face_coefficients(velocity, conduct, regime, opened):
    a = opened * velocity
    share = jnp.where(regime == 1.0, 0.5, jnp.where(velocity > 0.0, 0.0, 1.0))
    b = a * share - opened * conduct
    c = jnp.where(regime == 2.0, 0.5 * jnp.abs(a), 0.0)
    return a, b, c


def stage(source, target, kept, planes, north_flux, start, count, channels, levels, fold=None, patch=None):
    rows = pl.ds(start, count)
    volume = planes[6 * levels, rows]
    results = []
    for ch in range(channels):
        level = 6 * (ch % levels)

        def plane(i):
            return planes[level + i, rows]

        cell = source[ch, rows]
        behind = source[ch, pl.ds(start - 1, count)]
        ahead = source[ch, pl.ds(start + 1, count)]
        beyond = source[ch, pl.ds(start + 2, count)]
        north = face_flux(
            cell, ahead - cell, cell - behind, beyond - ahead, plane(3), plane(4), plane(5)
        )
        north_flux[ch, rows] = north
        if fold is not None:
            second, row = fold
            at = [source[ch, pl.ds(row + i, 8)] for i in (-2, -1, 0, 1)]
            theirs = face_flux(
                at[1],
                at[2] - at[1],
                at[1] - at[0],
                at[3] - at[2],
                *[second[3 * (ch % levels) + i] for i in range(3)],
            )
            north_flux[ch, pl.ds(row - 1, 1)] = theirs[0:1]
        east1 = pltpu.roll(cell, LANES - 1, 1)
        east2 = pltpu.roll(cell, LANES - 2, 1)
        west1 = pltpu.roll(cell, 1, 1)
        east = face_flux(
            cell,
            east1 - cell,
            cell - west1,
            east2 - east1,
            plane(0),
            plane(1),
            plane(2),
        )
        west = pltpu.roll(east, 1, 1)
        south = north_flux[ch, pl.ds(start - 1, count)]
        result = volume * ((west - east) + (south - north))
        if kept is None:
            result = cell + result
        else:
            result = 0.5 * ((kept[ch, rows] + cell) + result)
        if patch is not None:
            result = patch(result)
        target[ch, rows] = result
        results.append(result)
    return results


def unit(source, target, kept, planes, north_flux, ch, levels, start, count, fold, patch, results):
    rows, level = pl.ds(start, count), 6 * (ch % levels)
    cell = source[ch, rows]
    east1 = pltpu.roll(cell, LANES - 1, 1)
    west1 = pltpu.roll(cell, 1, 1)
    east2 = pltpu.roll(cell, LANES - 2, 1)
    yield
    behind = source[ch, pl.ds(start - 1, count)]
    ahead = source[ch, pl.ds(start + 1, count)]
    beyond = source[ch, pl.ds(start + 2, count)]
    north = face_flux(
        cell, ahead - cell, cell - behind, beyond - ahead, *[planes[level + i, rows] for i in (3, 4, 5)]
    )
    north_flux[ch, rows] = north
    if fold is not None and start <= fold[1] - 1 < start + count:
        second, row = fold
        at = [source[ch, pl.ds(row + i, 8)] for i in (-2, -1, 0, 1)]
        theirs = face_flux(
            at[1],
            at[2] - at[1],
            at[1] - at[0],
            at[3] - at[2],
            *[second[3 * (ch % levels) + i] for i in range(3)],
        )
        north_flux[ch, pl.ds(row - 1, 1)] = theirs[0:1]
    yield
    east = face_flux(
        cell, east1 - cell, cell - west1, east2 - east1, *[planes[level + i, rows] for i in range(3)]
    )
    west = pltpu.roll(east, 1, 1)
    yield
    south = north_flux[ch, pl.ds(start - 1, count)]
    result = planes[6 * levels, rows] * ((west - east) + (south - north))
    if kept is None:
        result = cell + result
    else:
        result = 0.5 * ((kept[ch, rows] + cell) + result)
    if patch is not None:
        result = patch(result, rows)
    target[ch, rows] = result
    results.append(result)


def pipeline(units):
    for turn in range(len(units) + 3):
        for phase in range(4):
            if 0 <= turn - phase < len(units):
                next(units[turn - phase], None)


def kernel(
    lon_count,
    lat_count,
    tracer,
    transport,
    diffusion,
    inverse_volume,
    sea_mask,
    regime,
    out,
    in_tracer,
    in_transport,
    in_diffusion,
    in_volume,
    in_mask,
    in_regime,
    mask,
    field,
    guess,
    planes,
    flux,
    packs,
    edges,
    lat_packs,
    lat_edges,
    lat_mask,
    lat_field,
    lat_guess,
    lat_planes,
    lat_flux,
    lat_second,
    lon_raw,
    lon_field,
    lon_guess,
    lon_planes,
    lon_flux,
    lon_second,
    patches,
    load_sem,
    lat_send,
    lat_recv,
    lon_send,
    lon_recv,
    corner_send,
    corner_recv,
):
    lon = lax.axis_index("lon")
    lat = lax.axis_index("lat")
    top = lat == lat_count - 1
    bottom = lat == 0
    left = lax.rem(lon + lon_count - 1, lon_count)
    right = lax.rem(lon + 1, lon_count)
    up = jnp.where(top, lat, lat + 1)
    up_lon = jnp.where(top, lon_count - 1 - lon, lon)
    up_left = jnp.where(top, lax.rem(lon_count - lon, lon_count), left)
    up_right = jnp.where(top, lax.rem(2 * lon_count - 2 - lon, lon_count), right)
    self_left = jnp.logical_and(top, up_left == lon)
    self_right = jnp.logical_and(top, up_right == lon)
    down = jnp.where(bottom, lat, lat - 1)

    barrier = pltpu.get_barrier_semaphore()

    def greet(to_lon, to_lat):
        pl.semaphore_signal(
            barrier, inc=1, device_id={"lon": to_lon, "lat": to_lat}, device_id_type=MESH
        )

    @pl.when(jnp.logical_not(self_left))
    def _():
        greet(up_left, up)

    @pl.when(jnp.logical_not(self_right))
    def _():
        greet(up_right, up)

    @pl.when(jnp.logical_not(bottom))
    def _():
        greet(left, down)
        greet(right, down)
        greet(lon, down)

    greet(up_lon, up)
    greet(left, lat)
    greet(right, lat)

    arrays = (tracer, transport, diffusion, inverse_volume, sea_mask, regime)
    held = (in_tracer, in_transport, in_diffusion, in_volume, in_mask, in_regime)
    loads = [pltpu.make_async_copy(a, h, load_sem.at[i]) for i, (a, h) in enumerate(zip(arrays, held))]
    for load in loads:
        load.start()

    pad = jnp.zeros((8, LANES), F32)
    for ref in (field, guess, flux, planes):
        for i in range(ref.shape[0]):
            ref[i, pl.ds(0, 8)] = pad
            ref[i, pl.ds(8 + ROWS, 8)] = pad
    mask[pl.ds(ROWS + 8, 8)] = pad
    for ref in (lat_field, lat_guess, lat_flux):
        for i in range(ref.shape[0]):
            ref[i, pl.ds(0, 8)] = pad
            ref[i, pl.ds(56, 8)] = pad
    for ref in (lon_field, lon_guess, lon_flux):
        ref[0, pl.ds(0, 8)] = pad
        ref[0, pl.ds(24 + ROWS, 8)] = pad
    lat_mask[pl.ds(56, 8)] = pad
    lon_raw[4, pl.ds(ROWS + 16, 8)] = pad
    for i in range(2):
        edges[i, pl.ds(ROWS + 16, 8)] = pad

    @pl.when(bottom)
    def _():
        lat_edges[0] = jnp.zeros(lat_edges.shape[1:], F32)
        for i in range(2):
            edges[i, pl.ds(0, 8)] = pad

    for load in loads:
        load.wait()

    lane, row8 = iota(8, 1), iota(8, 0)
    place, west_side = lane & 7, lane < 64
    own_cell = jnp.where(west_side, place, LANES - 1 - place)
    own_east = jnp.where(
        west_side, place, jnp.where((lane & 15) >= 8, LANES - 2 - place, LANES - 1)
    )
    level_lane = (lane >> 4) & 1
    sent_cell = jnp.where(west_side, LANES - 8 + place, 7 - place)
    sent_east = jnp.where(west_side, LANES - 8 + place, jnp.maximum(6 - place, 0))
    swapped_cell = jnp.where(west_side, 7 - place, LANES - 8 + place)
    swapped_east = jnp.where(west_side, jnp.maximum(6 - place, 0), LANES - 8 + place)

    def reflected(n):
        return jnp.where(iota(n, 1) < 64, 1.0, -1.0)

    def own_strips(cells, moves, steady):
        n = cells[0].shape[0]
        channel, odd = (iota(n, 1) >> 4) & 3, ((iota(n, 1) >> 4) & 1) == 1
        got = [lanes_of(a, own_cell) for a in cells]
        cell = got[0]
        for ch in range(1, CHANNELS):
            cell = jnp.where(channel == ch, got[ch], cell)
        speed_east = [lanes_of(a, own_east) for a in moves[:2]]
        speed_north = [lanes_of(a, own_cell) for a in moves[2:]]
        return cell, [
            jnp.where(odd, speed_east[1], speed_east[0]) * reflected(n),
            jnp.where(odd, speed_north[1], speed_north[0]),
            lanes_of(steady[0], own_east),
            lanes_of(steady[1], own_cell),
            lanes_of(steady[2], own_cell),
            lanes_of(steady[3], own_east),
            lanes_of(steady[4], own_cell),
            lanes_of(steady[2], own_next),
        ]

    own_next = jnp.where(west_side, place + 1, LANES - 2 - place)

    def tile_rows(r, n):
        rows = pl.ds(r, n)
        sea = in_mask[rows].astype(F32)
        cells = [in_tracer[ch // 2, ch % 2, rows] * sea for ch in range(CHANNELS)]
        moves = [in_transport[j // 2, j % 2, rows] for j in range(4)]
        steady = [in_diffusion[j, rows] for j in range(2)]
        steady += [in_volume[rows] * sea]
        steady += [in_regime[j, rows].astype(F32) for j in range(2)]
        return sea, cells, moves, steady

    for i, r in ((0, 0), (1, ROWS - 8)):
        _, cells, moves, steady = tile_rows(r, 8)
        for k, tile in enumerate(cells + moves + steady):
            lat_packs[i, k] = tile

    def pack(r, n):
        rows, padded = pl.ds(r, n), pl.ds(r + 8, n)
        sea, cells, moves, steady = tile_rows(r, n)
        mask[padded] = sea
        planes[12, padded] = steady[2]
        for ch in range(CHANNELS):
            field[ch, padded] = cells[ch]
        group, west_half = (iota(n, 1) >> 3) & 7, iota(n, 1) < 64
        first = lanes_of(cells[0], sent_cell)
        for ch in range(CHANNELS):
            if ch:
                first = jnp.where(group == 2 * ch, lanes_of(cells[ch], sent_cell), first)
            moved = lanes_of(moves[ch], sent_east if ch < 2 else sent_cell)
            first = jnp.where(group == 2 * ch + 1, moved * reflected(n) if ch < 2 else moved, first)
        second = lanes_of(steady[0], swapped_east)
        for k in range(1, 5):
            moved = lanes_of(steady[k], swapped_east if k == 3 else swapped_cell)
            second = jnp.where(group == k, moved, second)
        packs[0, rows] = jnp.where(west_half, second, first)
        packs[1, rows] = jnp.where(west_half, first, second)

    pack(0, ROWS)

    def remote(src, dst, send, recv, to_lon, to_lat):
        return pltpu.make_async_remote_copy(
            src_ref=src,
            dst_ref=dst,
            send_sem=send,
            recv_sem=recv,
            device_id={"lon": to_lon, "lat": to_lat},
            device_id_type=MESH,
        )

    to_left = remote(packs.at[0], edges.at[1, pl.ds(8, ROWS)], lon_send.at[0], lon_recv.at[1], left, lat)
    to_right = remote(packs.at[1], edges.at[0, pl.ds(8, ROWS)], lon_send.at[1], lon_recv.at[0], right, lat)
    corner_row = pl.multiple_of(jnp.where(top, ROWS + 8, 0), 8)
    top_int = top.astype(jnp.int32)
    corner_ul = remote(
        packs.at[0, pl.ds(ROWS - 8, 8)],
        edges.at[1 - top_int, pl.ds(corner_row, 8)],
        corner_send.at[0],
        corner_recv.at[1 + top_int],
        up_left,
        up,
    )
    corner_ur = remote(
        packs.at[1, pl.ds(ROWS - 8, 8)],
        edges.at[top_int, pl.ds(corner_row, 8)],
        corner_send.at[1],
        corner_recv.at[3 * top_int],
        up_right,
        up,
    )
    corner_dl = remote(
        packs.at[0, pl.ds(0, 8)],
        edges.at[1, pl.ds(ROWS + 8, 8)],
        corner_send.at[2],
        corner_recv.at[3],
        left,
        down,
    )
    corner_dr = remote(
        packs.at[1, pl.ds(0, 8)],
        edges.at[0, pl.ds(ROWS + 8, 8)],
        corner_send.at[3],
        corner_recv.at[2],
        right,
        down,
    )
    to_up = remote(
        lat_packs.at[1], lat_edges.at[top_int], lat_send.at[0], lat_recv.at[top_int], up_lon, up
    )
    to_down = remote(lat_packs.at[0], lat_edges.at[1], lat_send.at[1], lat_recv.at[1], lon, down)

    def dispatch():
        pl.semaphore_wait(
            barrier,
            5
            - self_left.astype(jnp.int32)
            - self_right.astype(jnp.int32)
            + 3 * jnp.logical_not(bottom).astype(jnp.int32),
        )

        @pl.when(jnp.logical_not(self_left))
        def _():
            corner_ul.start()

        @pl.when(jnp.logical_not(self_right))
        def _():
            corner_ur.start()

        to_up.start()

        @pl.when(jnp.logical_not(bottom))
        def _():
            corner_dl.start()
            corner_dr.start()
            to_down.start()

        to_left.start()
        to_right.start()

    early = lon == 0

    @pl.when(jnp.logical_not(early))
    def _():
        dispatch()

    @pl.when(self_left)
    def _():
        edges[0, pl.ds(ROWS + 8, 8)] = packs[0, pl.ds(ROWS - 8, 8)]

    @pl.when(self_right)
    def _():
        edges[1, pl.ds(ROWS + 8, 8)] = packs[1, pl.ds(ROWS - 8, 8)]

    def prepare(r, n):
        rows, padded = pl.ds(r, n), pl.ds(r + 8, n)
        sea = mask[padded]
        open_east = sea * pltpu.roll(sea, LANES - 1, 1)
        open_north = sea * mask[pl.ds(r + 9, n)]
        regimes = [in_regime[j, rows].astype(F32) for j in range(2)]
        moves = [in_transport[j // 2, j % 2, rows] for j in range(4)]
        steady = [in_diffusion[j, rows] for j in range(2)] + [planes[12, padded]] + regimes
        for level in range(2):
            for way, opened in ((0, open_east), (1, open_north)):
                found = face_coefficients(moves[2 * way + level], steady[way], regimes[way], opened)
                for j in range(3):
                    planes[6 * level + 3 * way + j, padded] = found[j]
        cell, raw = own_strips([field[ch, padded] for ch in range(CHANNELS)], moves, steady)
        lon_field[0, pl.ds(r + 16, n)] = cell
        for a, strip in enumerate(raw):
            lon_raw[a, padded] = strip

    for r in range(0, ROWS, PREP):
        prepare(r, PREP)

    for ch in range(CHANNELS):
        lat_field[ch, pl.ds(16, 16)] = field[ch, pl.ds(8, 16)]
        lat_field[ch, pl.ds(32, 16)] = field[ch, pl.ds(ROWS - 8, 16)]
    for i in range(13):
        lat_planes[i, pl.ds(16, 16)] = planes[i, pl.ds(8, 16)]
        lat_planes[i, pl.ds(32, 16)] = planes[i, pl.ds(ROWS - 8, 16)]
    lat_mask[pl.ds(16, 16)] = mask[pl.ds(8, 16)]
    lat_mask[pl.ds(32, 16)] = mask[pl.ds(ROWS - 8, 16)]

    before = (lane - 2) & (LANES - 1)
    inner = 6 + ((lane + 2) & 3)
    patch_column = jnp.where(before < 64, inner, LANES - 1 - inner)

    def patch_lanes(n):
        return ((iota(n, 1) + 2) & 15) < 4

    def patch_of(channels):
        n = channels[0].shape[0]
        channel = (((iota(n, 1) - 2) & (LANES - 1)) >> 4) & 3
        got = [lanes_of(a, patch_column) for a in channels]
        result = got[0]
        for ch in range(1, CHANNELS):
            result = jnp.where(channel == ch, got[ch], result)
        return result

    def interior(step, carry):
        def run(source, target, kept, k):
            def chunk(i, c):
                start = pl.multiple_of(i * INNER + 8, 8)
                results = stage(source, target, kept, planes, flux, start, INNER, CHANNELS, 2)
                patches[k, pl.ds(start, INNER)] = patch_of(results)
                return c

            lax.fori_loop(0, ROWS // INNER, chunk, 0)

        run(field, guess, None, 2 * step)
        run(guess, field, field, 2 * step + 1)
        return carry

    lax.fori_loop(0, STEPS, interior, 0)

    @pl.when(early)
    def _():
        dispatch()

    half = lane & 64
    far_index = [half + 16 * (j + level_lane) + 8 + place for j in (0, 2)]
    far_index += [(64 - half) + 8 * j + place for j in range(5)]

    def far_strips(west_edge, east_edge):
        west_half = iota(west_edge.shape[0], 1) < 64
        first = jnp.where(west_half, west_edge, east_edge)
        second = jnp.where(west_half, east_edge, west_edge)
        return first, [lanes_of(first if a < 2 else second, far_index[a]) for a in range(7)]

    def own_lanes(n, a):
        spot = iota(n, 1)
        if a in (0, 2, 5):
            return (spot & 15) >= jnp.where(spot < 64, 8, 7)
        return (spot & 15) >= 8

    def join(r, n):
        rows, padded = pl.ds(r, n), pl.ds(r + 8, n)
        whole = iota(n, 0) + r >= ROWS + 8
        whole_next = iota(n, 0) + r >= ROWS + 7
        west_edge, east_edge = edges[0, rows], edges[1, rows]
        first, far = far_strips(west_edge, east_edge)
        lon_field[0, padded] = jnp.where(
            jnp.logical_or(own_lanes(n, 1), whole), lon_field[0, padded], first
        )
        speed_east, speed_north, east_mix, north_mix, volume, east_rule, north_rule = [
            jnp.where(jnp.logical_or(own_lanes(n, a), whole), lon_raw[a, rows], far[a]) for a in range(7)
        ]
        lon_planes[6, padded] = volume
        ahead = pl.ds(r + 1, n)
        next_row = jnp.where(iota(n, 1) < 64, edges[1, ahead], edges[0, ahead])
        next_volume = jnp.where(
            jnp.logical_or(own_lanes(n, 4), whole_next),
            lon_raw[4, ahead],
            lanes_of(next_row, far_index[4]),
        )
        sea = jnp.where(volume > 0.0, 1.0, 0.0)
        sea_north = jnp.where(next_volume > 0.0, 1.0, 0.0)
        beyond_slot = jnp.where(lon_raw[7, rows] > 0.0, 1.0, 0.0)
        sea_east = jnp.where((iota(n, 1) & 15) == 15, beyond_slot, pltpu.roll(sea, LANES - 1, 1))
        found = face_coefficients(speed_east, east_mix, east_rule, sea * sea_east)
        found += face_coefficients(speed_north, north_mix, north_rule, sea * sea_north)
        for j in range(6):
            lon_planes[j, padded] = found[j]

    columns_first = jnp.logical_or(lon == 1, jnp.logical_not(jnp.logical_or(top, lat == lat_count // 2)))

    def columns():
        for side in range(2):
            remote(
                edges.at[side, pl.ds(8, ROWS)],
                edges.at[side, pl.ds(8, ROWS)],
                lon_send.at[0],
                lon_recv.at[side],
                lon,
                lat,
            ).wait_recv()

        join(8, 128)
        join(136, ROWS - 136)

    @pl.when(columns_first)
    def _():
        columns()

    remote(lat_edges.at[1], lat_edges.at[1], lat_send.at[0], lat_recv.at[1], lon, lat).wait_recv()

    @pl.when(jnp.logical_not(bottom))
    def _():
        remote(lat_edges.at[0], lat_edges.at[0], lat_send.at[0], lat_recv.at[0], lon, lat).wait_recv()

    below = [lat_edges[0, k] for k in range(SENT)]
    across = [lat_edges[1, k] for k in range(SENT)]
    norths = (6, 7, 9, 12)
    row_cell = jnp.where(top, 7 - row8, row8)
    row_north = jnp.where(top, jnp.maximum(6 - row8, 0), row8)
    sign = jnp.where(top, -1.0, 1.0)
    lane_cell = jnp.where(top, LANES - 1 - lane, lane)
    lane_east = jnp.where(top, jnp.maximum(LANES - 2 - lane, 0), lane)
    upper, second_raw = [], []
    for k in range(SENT):
        turned = lanes(across[k], lane_east if k in (4, 5, 8, 11) else lane_cell)
        if k in (4, 5, 6, 7):
            turned = turned * sign
        upper.append(sublanes(turned, row_north if k in norths else row_cell))
        if k in norths:
            second_raw.append(sublanes(turned, row_cell))

    lat_mask[pl.ds(8, 8)] = jnp.where(below[10] > 0.0, 1.0, 0.0)
    lat_mask[pl.ds(48, 8)] = jnp.where(upper[10] > 0.0, 1.0, 0.0)
    for ch in range(CHANNELS):
        lat_field[ch, pl.ds(8, 8)] = below[ch]
        lat_field[ch, pl.ds(48, 8)] = upper[ch]
    lat_planes[12, pl.ds(8, 8)] = below[10]
    lat_planes[12, pl.ds(48, 8)] = upper[10]
    highest = [lat_packs[1, k] for k in range(SENT)]
    for at, tiles in ((8, below), (40, highest), (48, upper)):
        sea = lat_mask[pl.ds(at, 8)]
        opened = (sea * pltpu.roll(sea, LANES - 1, 1), sea * lat_mask[pl.ds(at + 1, 8)])
        for level in range(2):
            for way in range(2):
                found = face_coefficients(
                    tiles[4 + 2 * way + level], tiles[8 + way], tiles[11 + way], opened[way]
                )
                for j in range(3):
                    lat_planes[6 * level + 3 * way + j, pl.ds(at, 8)] = found[j]

    opened = lat_mask[pl.ds(47, 8)] * lat_mask[pl.ds(48, 8)]
    for level in range(2):
        found = face_coefficients(second_raw[level], second_raw[2], second_raw[3], opened)
        for j in range(3):
            lat_second[3 * level + j] = jnp.where(top, found[j], lat_planes[6 * level + 3 + j, pl.ds(47, 8)])

    lat_pair, lon_pair = (lat_field, lat_guess), (lon_field, lon_guess)

    def lat_units(k, results):
        return [
            unit(
                lat_pair[k % 2],
                lat_pair[(k + 1) % 2],
                lat_field if k % 2 else None,
                lat_planes,
                lat_flux,
                ch,
                2,
                start,
                count,
                (lat_second, 48),
                None,
                results,
            )
            for ch in range(CHANNELS)
            for start, count in (((8, 48),) if k < 2 * STEPS - 1 else ((8, 16), (32, 16)))
        ]

    def lon_units(k):
        def patch(result, rows):
            n = result.shape[0]
            return jnp.where(patch_lanes(n), patches[k, pl.ds(rows.start - 8, n)], result)

        return [
            unit(
                lon_pair[k % 2],
                lon_pair[(k + 1) % 2],
                lon_field if k % 2 else None,
                lon_planes,
                lon_flux,
                0,
                1,
                8 + r,
                min(GROUP, ROWS + 16 - r),
                (lon_second, ROWS + 16),
                None if k == 2 * STEPS - 1 else patch,
                [],
            )
            for r in range(0, ROWS + 16, GROUP)
        ]

    def lat_done(k, results):
        if k < 2 * STEPS - 1:
            for at, to in ((0, 0), (32, ROWS)):
                patches[k, pl.ds(to, 16)] = patch_of([r[at : at + 16] for r in results])
        else:
            for ch in range(CHANNELS):
                field[ch, pl.ds(8, 8)] = lat_field[ch, pl.ds(16, 8)]
                field[ch, pl.ds(ROWS, 8)] = lat_field[ch, pl.ds(40, 8)]

    for k in range(2 * STEPS):
        results = []
        pipeline(lat_units(k, results))
        lat_done(k, results)

    @pl.when(jnp.logical_not(columns_first))
    def _():
        columns()

    @pl.when(jnp.logical_not(bottom))
    def _():
        for side in range(2):
            remote(
                edges.at[side, pl.ds(0, 8)],
                edges.at[side, pl.ds(0, 8)],
                corner_send.at[0],
                corner_recv.at[side],
                lon,
                lat,
            ).wait_recv()

    @pl.when(jnp.logical_not(self_left))
    def _():
        remote(
            edges.at[0, pl.ds(ROWS + 8, 8)],
            edges.at[0, pl.ds(ROWS + 8, 8)],
            corner_send.at[0],
            corner_recv.at[2],
            lon,
            lat,
        ).wait_recv()

    @pl.when(jnp.logical_not(self_right))
    def _():
        remote(
            edges.at[1, pl.ds(ROWS + 8, 8)],
            edges.at[1, pl.ds(ROWS + 8, 8)],
            corner_send.at[0],
            corner_recv.at[3],
            lon,
            lat,
        ).wait_recv()

    cell, raw = own_strips(below[:4], below[4:8], below[8:])
    lon_field[0, pl.ds(8, 8)] = cell
    for a, strip in enumerate(raw):
        lon_raw[a, pl.ds(0, 8)] = strip

    cell, raw = own_strips(across[:4], across[4:8], across[8:])
    corners = [edges[side, pl.ds(ROWS + 8, 8)] for side in range(2)]
    far_cell, far_raw = far_strips(
        jnp.where(top, corners[1], corners[0]), jnp.where(top, corners[0], corners[1])
    )
    side_swap = jnp.where(top, lane ^ 64, lane)
    cell = lanes(jnp.where(own_lanes(8, 1), cell, far_cell), side_swap)
    lon_field[0, pl.ds(ROWS + 16, 8)] = sublanes(cell, row_cell)
    second_raw = []
    for a in range(8):
        strip = raw[a] if a == 7 else jnp.where(own_lanes(8, a), raw[a], far_raw[a])
        turned = lanes(strip, side_swap)
        if a == 1:
            turned = turned * sign
        lon_raw[a, pl.ds(ROWS + 8, 8)] = sublanes(turned, row_north if a in (1, 3, 6) else row_cell)
        if a in (1, 3, 6):
            second_raw.append(sublanes(turned, row_cell))

    join(0, 8)
    join(ROWS, 16)

    seas = [jnp.where(lon_planes[6, pl.ds(ROWS + 15 + i, 8)] > 0.0, 1.0, 0.0) for i in range(2)]
    found = face_coefficients(*second_raw, seas[0] * seas[1])
    for j in range(3):
        lon_second[j] = jnp.where(top, found[j], lon_planes[3 + j, pl.ds(ROWS + 15, 8)])

    for k in range(2 * STEPS):
        pipeline(lon_units(k))

    def finish(r, n):
        rows, padded = pl.ds(r, n), pl.ds(r + 8, n)
        edge = lon_field[0, pl.ds(r + 16, n)]
        wide = iota(n, 1)
        kept = jnp.logical_and(wide >= 8, wide < LANES - 8)
        for ch in range(CHANNELS):
            index = 16 * ch + 8 + jnp.where(west_side, place, 64 + 7 - place)
            out[ch // 2, ch % 2, rows] = jnp.where(kept, field[ch, padded], lanes_of(edge, index))

    finish(0, ROWS)

    to_left.wait_send()
    to_right.wait_send()
    to_up.wait_send()

    @pl.when(jnp.logical_not(self_left))
    def _():
        corner_ul.wait_send()

    @pl.when(jnp.logical_not(self_right))
    def _():
        corner_ur.wait_send()

    @pl.when(jnp.logical_not(bottom))
    def _():
        corner_dl.wait_send()
        corner_dr.wait_send()
        to_down.wait_send()


def solution(mesh):
    lon_count, lat_count = mesh.shape["lon"], mesh.shape["lat"]
    placed = (
        P(None, None, "lat", "lon"),
        P(None, None, "lat", "lon"),
        P(None, "lat", "lon"),
        P("lat", "lon"),
        P("lat", "lon"),
        P(None, "lat", "lon"),
    )

    def local(*arrays):
        shapes = [a.shape for a in arrays]
        types = [a.dtype for a in arrays]
        tall, wide = ROWS + 16, ROWS + 32

        def vmem(*shape):
            return pltpu.VMEM(shape, F32)

        return pl.pallas_call(
            functools.partial(kernel, lon_count, lat_count),
            out_shape=pltpu.VMEM(shapes[0], F32),
            in_specs=[pl.BlockSpec(memory_space=pl.ANY)] * 6,
            out_specs=pl.BlockSpec(memory_space=pltpu.VMEM),
            scratch_shapes=[
                *[pltpu.VMEM(s, t) for s, t in zip(shapes, types)],
                vmem(tall, LANES),
                vmem(CHANNELS, tall, LANES),
                vmem(CHANNELS, tall, LANES),
                vmem(13, tall, LANES),
                vmem(CHANNELS, tall, LANES),
                vmem(2, ROWS, LANES),
                vmem(2, tall + 8, LANES),
                vmem(2, SENT, 8, LANES),
                vmem(2, SENT, 8, LANES),
                vmem(64, LANES),
                vmem(CHANNELS, 64, LANES),
                vmem(CHANNELS, 64, LANES),
                vmem(13, 64, LANES),
                vmem(CHANNELS, 64, LANES),
                vmem(6, 8, LANES),
                vmem(8, tall + 8, LANES),
                vmem(1, wide, LANES),
                vmem(1, wide, LANES),
                vmem(7, wide, LANES),
                vmem(1, wide, LANES),
                vmem(3, 8, LANES),
                vmem(2 * STEPS, tall, LANES),
                pltpu.SemaphoreType.DMA((6,)),
                pltpu.SemaphoreType.DMA((2,)),
                pltpu.SemaphoreType.DMA((2,)),
                pltpu.SemaphoreType.DMA((2,)),
                pltpu.SemaphoreType.DMA((2,)),
                pltpu.SemaphoreType.DMA((4,)),
                pltpu.SemaphoreType.DMA((4,)),
            ],
            compiler_params=pltpu.CompilerParams(
                collective_id=0, has_side_effects=True, vmem_limit_bytes=64900 * 1024
            ),
        )(*arrays)

    return jax.shard_map(
        local, mesh=mesh, in_specs=placed, out_specs=P(None, None, "lat", "lon"), check_vma=False
    )
```

```python
import functools

import jax
import jax.numpy as jnp
from jax import lax
from jax.experimental import pallas as pl
from jax.experimental.pallas import tpu as pltpu
from jax.sharding import PartitionSpec as P

STEPS = 2
MESH = pl.DeviceIdType.MESH
HALO = 8
ROWS = 256
LANES = 128
CHANNELS = 4
F32 = jnp.float32
INNER = 256
PREP = 64
GROUP = 72

SENT = 13


def iota(rows, axis):
    return lax.broadcasted_iota(jnp.int32, (rows, LANES), axis)


def lanes(tile, index):
    return jnp.take_along_axis(tile, index, axis=1, mode="promise_in_bounds")


def sublanes(tile, index):
    return jnp.take_along_axis(tile, index, axis=0, mode="promise_in_bounds")


def lanes_of(rows, index):
    tiles = [lanes(rows[8 * i : 8 * i + 8], index) for i in range(rows.shape[0] // 8)]
    return tiles[0] if len(tiles) == 1 else jnp.concatenate(tiles, axis=0)


def face_flux(cell, gap, gap_behind, gap_beyond, a, b, c):
    other = jnp.where(a > 0.0, gap_behind, gap_beyond)
    slope = jnp.maximum(jnp.minimum(gap, 0.0), jnp.minimum(other, jnp.maximum(gap, 0.0)))
    return a * cell + b * gap + c * slope


def face_coefficients(velocity, conduct, regime, opened):
    a = opened * velocity
    share = jnp.where(regime == 1.0, 0.5, jnp.where(velocity > 0.0, 0.0, 1.0))
    b = a * share - opened * conduct
    c = jnp.where(regime == 2.0, 0.5 * jnp.abs(a), 0.0)
    return a, b, c


def stage(source, target, kept, planes, north_flux, start, count, channels, levels, fold=None, patch=None):
    rows = pl.ds(start, count)
    volume = planes[6 * levels, rows]
    results = []
    for ch in range(channels):
        level = 6 * (ch % levels)

        def plane(i):
            return planes[level + i, rows]

        cell = source[ch, rows]
        behind = source[ch, pl.ds(start - 1, count)]
        ahead = source[ch, pl.ds(start + 1, count)]
        beyond = source[ch, pl.ds(start + 2, count)]
        north = face_flux(
            cell, ahead - cell, cell - behind, beyond - ahead, plane(3), plane(4), plane(5)
        )
        north_flux[ch, rows] = north
        if fold is not None:
            second, row = fold
            at = [source[ch, pl.ds(row + i, 8)] for i in (-2, -1, 0, 1)]
            theirs = face_flux(
                at[1],
                at[2] - at[1],
                at[1] - at[0],
                at[3] - at[2],
                *[second[3 * (ch % levels) + i] for i in range(3)],
            )
            north_flux[ch, pl.ds(row - 1, 1)] = theirs[0:1]
        east1 = pltpu.roll(cell, LANES - 1, 1)
        east2 = pltpu.roll(cell, LANES - 2, 1)
        west1 = pltpu.roll(cell, 1, 1)
        east = face_flux(
            cell,
            east1 - cell,
            cell - west1,
            east2 - east1,
            plane(0),
            plane(1),
            plane(2),
        )
        west = pltpu.roll(east, 1, 1)
        south = north_flux[ch, pl.ds(start - 1, count)]
        result = volume * ((west - east) + (south - north))
        if kept is None:
            result = cell + result
        else:
            result = 0.5 * ((kept[ch, rows] + cell) + result)
        if patch is not None:
            result = patch(result)
        target[ch, rows] = result
        results.append(result)
    return results


def unit(source, target, kept, planes, north_flux, ch, levels, start, count, fold, patch, results):
    rows, level = pl.ds(start, count), 6 * (ch % levels)
    cell = source[ch, rows]
    east1 = pltpu.roll(cell, LANES - 1, 1)
    west1 = pltpu.roll(cell, 1, 1)
    east2 = pltpu.roll(cell, LANES - 2, 1)
    yield
    behind = source[ch, pl.ds(start - 1, count)]
    ahead = source[ch, pl.ds(start + 1, count)]
    beyond = source[ch, pl.ds(start + 2, count)]
    north = face_flux(
        cell, ahead - cell, cell - behind, beyond - ahead, *[planes[level + i, rows] for i in (3, 4, 5)]
    )
    north_flux[ch, rows] = north
    if fold is not None and start <= fold[1] - 1 < start + count:
        second, row = fold
        at = [source[ch, pl.ds(row + i, 8)] for i in (-2, -1, 0, 1)]
        theirs = face_flux(
            at[1],
            at[2] - at[1],
            at[1] - at[0],
            at[3] - at[2],
            *[second[3 * (ch % levels) + i] for i in range(3)],
        )
        north_flux[ch, pl.ds(row - 1, 1)] = theirs[0:1]
    yield
    east = face_flux(
        cell, east1 - cell, cell - west1, east2 - east1, *[planes[level + i, rows] for i in range(3)]
    )
    west = pltpu.roll(east, 1, 1)
    yield
    south = north_flux[ch, pl.ds(start - 1, count)]
    result = planes[6 * levels, rows] * ((west - east) + (south - north))
    if kept is None:
        result = cell + result
    else:
        result = 0.5 * ((kept[ch, rows] + cell) + result)
    if patch is not None:
        result = patch(result, rows)
    target[ch, rows] = result
    results.append(result)


def pipeline(units):
    for turn in range(len(units) + 3):
        for phase in range(4):
            if 0 <= turn - phase < len(units):
                next(units[turn - phase], None)


def kernel(
    lon_count,
    lat_count,
    tracer,
    transport,
    diffusion,
    inverse_volume,
    sea_mask,
    regime,
    out,
    in_tracer,
    in_transport,
    in_diffusion,
    in_volume,
    in_mask,
    in_regime,
    mask,
    field,
    guess,
    planes,
    flux,
    packs,
    edges,
    lat_packs,
    lat_edges,
    lat_mask,
    lat_field,
    lat_guess,
    lat_planes,
    lat_flux,
    lat_second,
    lon_raw,
    lon_field,
    lon_guess,
    lon_planes,
    lon_flux,
    lon_second,
    patches,
    load_sem,
    lat_send,
    lat_recv,
    lon_send,
    lon_recv,
    corner_send,
    corner_recv,
):
    lon = lax.axis_index("lon")
    lat = lax.axis_index("lat")
    top = lat == lat_count - 1
    bottom = lat == 0
    left = lax.rem(lon + lon_count - 1, lon_count)
    right = lax.rem(lon + 1, lon_count)
    up = jnp.where(top, lat, lat + 1)
    up_lon = jnp.where(top, lon_count - 1 - lon, lon)
    up_left = jnp.where(top, lax.rem(lon_count - lon, lon_count), left)
    up_right = jnp.where(top, lax.rem(2 * lon_count - 2 - lon, lon_count), right)
    self_left = jnp.logical_and(top, up_left == lon)
    self_right = jnp.logical_and(top, up_right == lon)
    down = jnp.where(bottom, lat, lat - 1)

    barrier = pltpu.get_barrier_semaphore()

    def greet(to_lon, to_lat):
        pl.semaphore_signal(
            barrier, inc=1, device_id={"lon": to_lon, "lat": to_lat}, device_id_type=MESH
        )

    @pl.when(jnp.logical_not(self_left))
    def _():
        greet(up_left, up)

    @pl.when(jnp.logical_not(self_right))
    def _():
        greet(up_right, up)

    @pl.when(jnp.logical_not(bottom))
    def _():
        greet(left, down)
        greet(right, down)
        greet(lon, down)

    greet(up_lon, up)
    greet(left, lat)
    greet(right, lat)

    arrays = (tracer, transport, diffusion, inverse_volume, sea_mask, regime)
    held = (in_tracer, in_transport, in_diffusion, in_volume, in_mask, in_regime)
    loads = [pltpu.make_async_copy(a, h, load_sem.at[i]) for i, (a, h) in enumerate(zip(arrays, held))]
    for load in loads:
        load.start()

    pad = jnp.zeros((8, LANES), F32)
    for ref in (field, guess, flux, planes):
        for i in range(ref.shape[0]):
            ref[i, pl.ds(0, 8)] = pad
            ref[i, pl.ds(8 + ROWS, 8)] = pad
    mask[pl.ds(ROWS + 8, 8)] = pad
    for ref in (lat_field, lat_guess, lat_flux):
        for i in range(ref.shape[0]):
            ref[i, pl.ds(0, 8)] = pad
            ref[i, pl.ds(56, 8)] = pad
    for ref in (lon_field, lon_guess, lon_flux):
        ref[0, pl.ds(0, 8)] = pad
        ref[0, pl.ds(24 + ROWS, 8)] = pad
    lat_mask[pl.ds(56, 8)] = pad
    lon_raw[4, pl.ds(ROWS + 16, 8)] = pad
    for i in range(2):
        edges[i, pl.ds(ROWS + 16, 8)] = pad

    @pl.when(bottom)
    def _():
        lat_edges[0] = jnp.zeros(lat_edges.shape[1:], F32)
        for i in range(2):
            edges[i, pl.ds(0, 8)] = pad

    for load in loads:
        load.wait()

    lane, row8 = iota(8, 1), iota(8, 0)
    place, west_side = lane & 7, lane < 64
    own_cell = jnp.where(west_side, place, LANES - 1 - place)
    own_east = jnp.where(
        west_side, place, jnp.where((lane & 15) >= 8, LANES - 2 - place, LANES - 1)
    )
    level_lane = (lane >> 4) & 1
    sent_cell = jnp.where(west_side, LANES - 8 + place, 7 - place)
    sent_east = jnp.where(west_side, LANES - 8 + place, jnp.maximum(6 - place, 0))
    swapped_cell = jnp.where(west_side, 7 - place, LANES - 8 + place)
    swapped_east = jnp.where(west_side, jnp.maximum(6 - place, 0), LANES - 8 + place)

    def reflected(n):
        return jnp.where(iota(n, 1) < 64, 1.0, -1.0)

    def own_strips(cells, moves, steady):
        n = cells[0].shape[0]
        channel, odd = (iota(n, 1) >> 4) & 3, ((iota(n, 1) >> 4) & 1) == 1
        got = [lanes_of(a, own_cell) for a in cells]
        cell = got[0]
        for ch in range(1, CHANNELS):
            cell = jnp.where(channel == ch, got[ch], cell)
        speed_east = [lanes_of(a, own_east) for a in moves[:2]]
        speed_north = [lanes_of(a, own_cell) for a in moves[2:]]
        return cell, [
            jnp.where(odd, speed_east[1], speed_east[0]) * reflected(n),
            jnp.where(odd, speed_north[1], speed_north[0]),
            lanes_of(steady[0], own_east),
            lanes_of(steady[1], own_cell),
            lanes_of(steady[2], own_cell),
            lanes_of(steady[3], own_east),
            lanes_of(steady[4], own_cell),
            lanes_of(steady[2], own_next),
        ]

    own_next = jnp.where(west_side, place + 1, LANES - 2 - place)

    def tile_rows(r, n):
        rows = pl.ds(r, n)
        sea = in_mask[rows].astype(F32)
        cells = [in_tracer[ch // 2, ch % 2, rows] * sea for ch in range(CHANNELS)]
        moves = [in_transport[j // 2, j % 2, rows] for j in range(4)]
        steady = [in_diffusion[j, rows] for j in range(2)]
        steady += [in_volume[rows] * sea]
        steady += [in_regime[j, rows].astype(F32) for j in range(2)]
        return sea, cells, moves, steady

    for i, r in ((0, 0), (1, ROWS - 8)):
        _, cells, moves, steady = tile_rows(r, 8)
        for k, tile in enumerate(cells + moves + steady):
            lat_packs[i, k] = tile

    def pack(r, n):
        rows, padded = pl.ds(r, n), pl.ds(r + 8, n)
        sea, cells, moves, steady = tile_rows(r, n)
        mask[padded] = sea
        planes[12, padded] = steady[2]
        for ch in range(CHANNELS):
            field[ch, padded] = cells[ch]
        group, west_half = (iota(n, 1) >> 3) & 7, iota(n, 1) < 64
        first = lanes_of(cells[0], sent_cell)
        for ch in range(CHANNELS):
            if ch:
                first = jnp.where(group == 2 * ch, lanes_of(cells[ch], sent_cell), first)
            moved = lanes_of(moves[ch], sent_east if ch < 2 else sent_cell)
            first = jnp.where(group == 2 * ch + 1, moved * reflected(n) if ch < 2 else moved, first)
        second = lanes_of(steady[0], swapped_east)
        for k in range(1, 5):
            moved = lanes_of(steady[k], swapped_east if k == 3 else swapped_cell)
            second = jnp.where(group == k, moved, second)
        packs[0, rows] = jnp.where(west_half, second, first)
        packs[1, rows] = jnp.where(west_half, first, second)

    pack(0, ROWS)

    def remote(src, dst, send, recv, to_lon, to_lat):
        return pltpu.make_async_remote_copy(
            src_ref=src,
            dst_ref=dst,
            send_sem=send,
            recv_sem=recv,
            device_id={"lon": to_lon, "lat": to_lat},
            device_id_type=MESH,
        )

    to_left = remote(packs.at[0], edges.at[1, pl.ds(8, ROWS)], lon_send.at[0], lon_recv.at[1], left, lat)
    to_right = remote(packs.at[1], edges.at[0, pl.ds(8, ROWS)], lon_send.at[1], lon_recv.at[0], right, lat)
    corner_row = pl.multiple_of(jnp.where(top, ROWS + 8, 0), 8)
    top_int = top.astype(jnp.int32)
    corner_ul = remote(
        packs.at[0, pl.ds(ROWS - 8, 8)],
        edges.at[1 - top_int, pl.ds(corner_row, 8)],
        corner_send.at[0],
        corner_recv.at[1 + top_int],
        up_left,
        up,
    )
    corner_ur = remote(
        packs.at[1, pl.ds(ROWS - 8, 8)],
        edges.at[top_int, pl.ds(corner_row, 8)],
        corner_send.at[1],
        corner_recv.at[3 * top_int],
        up_right,
        up,
    )
    corner_dl = remote(
        packs.at[0, pl.ds(0, 8)],
        edges.at[1, pl.ds(ROWS + 8, 8)],
        corner_send.at[2],
        corner_recv.at[3],
        left,
        down,
    )
    corner_dr = remote(
        packs.at[1, pl.ds(0, 8)],
        edges.at[0, pl.ds(ROWS + 8, 8)],
        corner_send.at[3],
        corner_recv.at[2],
        right,
        down,
    )
    to_up = remote(
        lat_packs.at[1], lat_edges.at[top_int], lat_send.at[0], lat_recv.at[top_int], up_lon, up
    )
    to_down = remote(lat_packs.at[0], lat_edges.at[1], lat_send.at[1], lat_recv.at[1], lon, down)

    def dispatch():
        pl.semaphore_wait(
            barrier,
            5
            - self_left.astype(jnp.int32)
            - self_right.astype(jnp.int32)
            + 3 * jnp.logical_not(bottom).astype(jnp.int32),
        )

        @pl.when(jnp.logical_not(self_left))
        def _():
            corner_ul.start()

        @pl.when(jnp.logical_not(self_right))
        def _():
            corner_ur.start()

        to_up.start()

        @pl.when(jnp.logical_not(bottom))
        def _():
            corner_dl.start()
            corner_dr.start()
            to_down.start()

        to_left.start()
        to_right.start()

    early = lon == 0

    @pl.when(jnp.logical_not(early))
    def _():
        dispatch()

    @pl.when(self_left)
    def _():
        edges[0, pl.ds(ROWS + 8, 8)] = packs[0, pl.ds(ROWS - 8, 8)]

    @pl.when(self_right)
    def _():
        edges[1, pl.ds(ROWS + 8, 8)] = packs[1, pl.ds(ROWS - 8, 8)]

    def prepare(r, n):
        rows, padded = pl.ds(r, n), pl.ds(r + 8, n)
        sea = mask[padded]
        open_east = sea * pltpu.roll(sea, LANES - 1, 1)
        open_north = sea * mask[pl.ds(r + 9, n)]
        regimes = [in_regime[j, rows].astype(F32) for j in range(2)]
        moves = [in_transport[j // 2, j % 2, rows] for j in range(4)]
        steady = [in_diffusion[j, rows] for j in range(2)] + [planes[12, padded]] + regimes
        for level in range(2):
            for way, opened in ((0, open_east), (1, open_north)):
                found = face_coefficients(moves[2 * way + level], steady[way], regimes[way], opened)
                for j in range(3):
                    planes[6 * level + 3 * way + j, padded] = found[j]
        cell, raw = own_strips([field[ch, padded] for ch in range(CHANNELS)], moves, steady)
        lon_field[0, pl.ds(r + 16, n)] = cell
        for a, strip in enumerate(raw):
            lon_raw[a, padded] = strip

    for r in range(0, ROWS, PREP):
        prepare(r, PREP)

    for ch in range(CHANNELS):
        lat_field[ch, pl.ds(16, 16)] = field[ch, pl.ds(8, 16)]
        lat_field[ch, pl.ds(32, 16)] = field[ch, pl.ds(ROWS - 8, 16)]
    for i in range(13):
        lat_planes[i, pl.ds(16, 16)] = planes[i, pl.ds(8, 16)]
        lat_planes[i, pl.ds(32, 16)] = planes[i, pl.ds(ROWS - 8, 16)]
    lat_mask[pl.ds(16, 16)] = mask[pl.ds(8, 16)]
    lat_mask[pl.ds(32, 16)] = mask[pl.ds(ROWS - 8, 16)]

    before = (lane - 2) & (LANES - 1)
    inner = 6 + ((lane + 2) & 3)
    patch_column = jnp.where(before < 64, inner, LANES - 1 - inner)

    def patch_lanes(n):
        return ((iota(n, 1) + 2) & 15) < 4

    def patch_of(channels):
        n = channels[0].shape[0]
        channel = (((iota(n, 1) - 2) & (LANES - 1)) >> 4) & 3
        got = [lanes_of(a, patch_column) for a in channels]
        result = got[0]
        for ch in range(1, CHANNELS):
            result = jnp.where(channel == ch, got[ch], result)
        return result

    def interior(step, carry):
        def run(source, target, kept, k):
            def chunk(i, c):
                start = pl.multiple_of(i * INNER + 8, 8)
                results = stage(source, target, kept, planes, flux, start, INNER, CHANNELS, 2)
                patches[k, pl.ds(start, INNER)] = patch_of(results)
                return c

            lax.fori_loop(0, ROWS // INNER, chunk, 0)

        run(field, guess, None, 2 * step)
        run(guess, field, field, 2 * step + 1)
        return carry

    lax.fori_loop(0, STEPS, interior, 0)

    @pl.when(early)
    def _():
        dispatch()

    half = lane & 64
    far_index = [half + 16 * (j + level_lane) + 8 + place for j in (0, 2)]
    far_index += [(64 - half) + 8 * j + place for j in range(5)]

    def far_strips(west_edge, east_edge):
        west_half = iota(west_edge.shape[0], 1) < 64
        first = jnp.where(west_half, west_edge, east_edge)
        second = jnp.where(west_half, east_edge, west_edge)
        return first, [lanes_of(first if a < 2 else second, far_index[a]) for a in range(7)]

    def own_lanes(n, a):
        spot = iota(n, 1)
        if a in (0, 2, 5):
            return (spot & 15) >= jnp.where(spot < 64, 8, 7)
        return (spot & 15) >= 8

    def join(r, n):
        rows, padded = pl.ds(r, n), pl.ds(r + 8, n)
        whole = iota(n, 0) + r >= ROWS + 8
        whole_next = iota(n, 0) + r >= ROWS + 7
        west_edge, east_edge = edges[0, rows], edges[1, rows]
        first, far = far_strips(west_edge, east_edge)
        lon_field[0, padded] = jnp.where(
            jnp.logical_or(own_lanes(n, 1), whole), lon_field[0, padded], first
        )
        speed_east, speed_north, east_mix, north_mix, volume, east_rule, north_rule = [
            jnp.where(jnp.logical_or(own_lanes(n, a), whole), lon_raw[a, rows], far[a]) for a in range(7)
        ]
        lon_planes[6, padded] = volume
        ahead = pl.ds(r + 1, n)
        next_row = jnp.where(iota(n, 1) < 64, edges[1, ahead], edges[0, ahead])
        next_volume = jnp.where(
            jnp.logical_or(own_lanes(n, 4), whole_next),
            lon_raw[4, ahead],
            lanes_of(next_row, far_index[4]),
        )
        sea = jnp.where(volume > 0.0, 1.0, 0.0)
        sea_north = jnp.where(next_volume > 0.0, 1.0, 0.0)
        beyond_slot = jnp.where(lon_raw[7, rows] > 0.0, 1.0, 0.0)
        sea_east = jnp.where((iota(n, 1) & 15) == 15, beyond_slot, pltpu.roll(sea, LANES - 1, 1))
        found = face_coefficients(speed_east, east_mix, east_rule, sea * sea_east)
        found += face_coefficients(speed_north, north_mix, north_rule, sea * sea_north)
        for j in range(6):
            lon_planes[j, padded] = found[j]

    columns_first = jnp.logical_or(lon == 1, jnp.logical_not(jnp.logical_or(top, lat == lat_count // 2)))

    def columns():
        for side in range(2):
            remote(
                edges.at[side, pl.ds(8, ROWS)],
                edges.at[side, pl.ds(8, ROWS)],
                lon_send.at[0],
                lon_recv.at[side],
                lon,
                lat,
            ).wait_recv()

        join(8, 128)
        join(136, ROWS - 136)

    @pl.when(columns_first)
    def _():
        columns()

    remote(lat_edges.at[1], lat_edges.at[1], lat_send.at[0], lat_recv.at[1], lon, lat).wait_recv()

    @pl.when(jnp.logical_not(bottom))
    def _():
        remote(lat_edges.at[0], lat_edges.at[0], lat_send.at[0], lat_recv.at[0], lon, lat).wait_recv()

    below = [lat_edges[0, k] for k in range(SENT)]
    across = [lat_edges[1, k] for k in range(SENT)]
    norths = (6, 7, 9, 12)
    row_cell = jnp.where(top, 7 - row8, row8)
    row_north = jnp.where(top, jnp.maximum(6 - row8, 0), row8)
    sign = jnp.where(top, -1.0, 1.0)
    lane_cell = jnp.where(top, LANES - 1 - lane, lane)
    lane_east = jnp.where(top, jnp.maximum(LANES - 2 - lane, 0), lane)
    upper, second_raw = [], []
    for k in range(SENT):
        turned = lanes(across[k], lane_east if k in (4, 5, 8, 11) else lane_cell)
        if k in (4, 5, 6, 7):
            turned = turned * sign
        upper.append(sublanes(turned, row_north if k in norths else row_cell))
        if k in norths:
            second_raw.append(sublanes(turned, row_cell))

    lat_mask[pl.ds(8, 8)] = jnp.where(below[10] > 0.0, 1.0, 0.0)
    lat_mask[pl.ds(48, 8)] = jnp.where(upper[10] > 0.0, 1.0, 0.0)
    for ch in range(CHANNELS):
        lat_field[ch, pl.ds(8, 8)] = below[ch]
        lat_field[ch, pl.ds(48, 8)] = upper[ch]
    lat_planes[12, pl.ds(8, 8)] = below[10]
    lat_planes[12, pl.ds(48, 8)] = upper[10]
    highest = [lat_packs[1, k] for k in range(SENT)]
    for at, tiles in ((8, below), (40, highest), (48, upper)):
        sea = lat_mask[pl.ds(at, 8)]
        opened = (sea * pltpu.roll(sea, LANES - 1, 1), sea * lat_mask[pl.ds(at + 1, 8)])
        for level in range(2):
            for way in range(2):
                found = face_coefficients(
                    tiles[4 + 2 * way + level], tiles[8 + way], tiles[11 + way], opened[way]
                )
                for j in range(3):
                    lat_planes[6 * level + 3 * way + j, pl.ds(at, 8)] = found[j]

    opened = lat_mask[pl.ds(47, 8)] * lat_mask[pl.ds(48, 8)]
    for level in range(2):
        found = face_coefficients(second_raw[level], second_raw[2], second_raw[3], opened)
        for j in range(3):
            lat_second[3 * level + j] = jnp.where(top, found[j], lat_planes[6 * level + 3 + j, pl.ds(47, 8)])

    cell, raw = own_strips(below[:4], below[4:8], below[8:])
    lon_field[0, pl.ds(8, 8)] = cell
    for a, strip in enumerate(raw):
        lon_raw[a, pl.ds(0, 8)] = strip

    own_across = own_strips(across[:4], across[4:8], across[8:])

    lat_pair, lon_pair = (lat_field, lat_guess), (lon_field, lon_guess)

    def lat_units(k, results):
        return [
            unit(
                lat_pair[k % 2],
                lat_pair[(k + 1) % 2],
                lat_field if k % 2 else None,
                lat_planes,
                lat_flux,
                ch,
                2,
                start,
                count,
                (lat_second, 48),
                None,
                results,
            )
            for ch in range(CHANNELS)
            for start, count in (((8, 48),) if k < 2 * STEPS - 1 else ((8, 16), (32, 16)))
        ]

    def lon_units(k):
        def patch(result, rows):
            n = result.shape[0]
            return jnp.where(patch_lanes(n), patches[k, pl.ds(rows.start - 8, n)], result)

        return [
            unit(
                lon_pair[k % 2],
                lon_pair[(k + 1) % 2],
                lon_field if k % 2 else None,
                lon_planes,
                lon_flux,
                0,
                1,
                8 + r,
                min(GROUP, ROWS + 16 - r),
                (lon_second, ROWS + 16),
                None if k == 2 * STEPS - 1 else patch,
                [],
            )
            for r in range(0, ROWS + 16, GROUP)
        ]

    def lat_done(k, results):
        if k < 2 * STEPS - 1:
            for at, to in ((0, 0), (32, ROWS)):
                patches[k, pl.ds(to, 16)] = patch_of([r[at : at + 16] for r in results])
        else:
            for ch in range(CHANNELS):
                field[ch, pl.ds(8, 8)] = lat_field[ch, pl.ds(16, 8)]
                field[ch, pl.ds(ROWS, 8)] = lat_field[ch, pl.ds(40, 8)]

    for k in range(2 * STEPS):
        results = []
        pipeline(lat_units(k, results))
        lat_done(k, results)

    @pl.when(jnp.logical_not(columns_first))
    def _():
        columns()

    @pl.when(jnp.logical_not(bottom))
    def _():
        for side in range(2):
            remote(
                edges.at[side, pl.ds(0, 8)],
                edges.at[side, pl.ds(0, 8)],
                corner_send.at[0],
                corner_recv.at[side],
                lon,
                lat,
            ).wait_recv()

    @pl.when(jnp.logical_not(self_left))
    def _():
        remote(
            edges.at[0, pl.ds(ROWS + 8, 8)],
            edges.at[0, pl.ds(ROWS + 8, 8)],
            corner_send.at[0],
            corner_recv.at[2],
            lon,
            lat,
        ).wait_recv()

    @pl.when(jnp.logical_not(self_right))
    def _():
        remote(
            edges.at[1, pl.ds(ROWS + 8, 8)],
            edges.at[1, pl.ds(ROWS + 8, 8)],
            corner_send.at[0],
            corner_recv.at[3],
            lon,
            lat,
        ).wait_recv()

    cell, raw = own_across
    corners = [edges[side, pl.ds(ROWS + 8, 8)] for side in range(2)]
    far_cell, far_raw = far_strips(
        jnp.where(top, corners[1], corners[0]), jnp.where(top, corners[0], corners[1])
    )
    side_swap = jnp.where(top, lane ^ 64, lane)
    cell = lanes(jnp.where(own_lanes(8, 1), cell, far_cell), side_swap)
    lon_field[0, pl.ds(ROWS + 16, 8)] = sublanes(cell, row_cell)
    second_raw = []
    for a in range(8):
        strip = raw[a] if a == 7 else jnp.where(own_lanes(8, a), raw[a], far_raw[a])
        turned = lanes(strip, side_swap)
        if a == 1:
            turned = turned * sign
        lon_raw[a, pl.ds(ROWS + 8, 8)] = sublanes(turned, row_north if a in (1, 3, 6) else row_cell)
        if a in (1, 3, 6):
            second_raw.append(sublanes(turned, row_cell))

    join(0, 8)
    join(ROWS, 16)

    seas = [jnp.where(lon_planes[6, pl.ds(ROWS + 15 + i, 8)] > 0.0, 1.0, 0.0) for i in range(2)]
    found = face_coefficients(*second_raw, seas[0] * seas[1])
    for j in range(3):
        lon_second[j] = jnp.where(top, found[j], lon_planes[3 + j, pl.ds(ROWS + 15, 8)])

    for k in range(2 * STEPS):
        pipeline(lon_units(k))

    def finish(r, n):
        rows, padded = pl.ds(r, n), pl.ds(r + 8, n)
        edge = lon_field[0, pl.ds(r + 16, n)]
        wide = iota(n, 1)
        kept = jnp.logical_and(wide >= 8, wide < LANES - 8)
        for ch in range(CHANNELS):
            index = 16 * ch + 8 + jnp.where(west_side, place, 64 + 7 - place)
            out[ch // 2, ch % 2, rows] = jnp.where(kept, field[ch, padded], lanes_of(edge, index))

    finish(0, ROWS)

    to_left.wait_send()
    to_right.wait_send()
    to_up.wait_send()

    @pl.when(jnp.logical_not(self_left))
    def _():
        corner_ul.wait_send()

    @pl.when(jnp.logical_not(self_right))
    def _():
        corner_ur.wait_send()

    @pl.when(jnp.logical_not(bottom))
    def _():
        corner_dl.wait_send()
        corner_dr.wait_send()
        to_down.wait_send()


def solution(mesh):
    lon_count, lat_count = mesh.shape["lon"], mesh.shape["lat"]
    placed = (
        P(None, None, "lat", "lon"),
        P(None, None, "lat", "lon"),
        P(None, "lat", "lon"),
        P("lat", "lon"),
        P("lat", "lon"),
        P(None, "lat", "lon"),
    )

    def local(*arrays):
        shapes = [a.shape for a in arrays]
        types = [a.dtype for a in arrays]
        tall, wide = ROWS + 16, ROWS + 32

        def vmem(*shape):
            return pltpu.VMEM(shape, F32)

        return pl.pallas_call(
            functools.partial(kernel, lon_count, lat_count),
            out_shape=pltpu.VMEM(shapes[0], F32),
            in_specs=[pl.BlockSpec(memory_space=pl.ANY)] * 6,
            out_specs=pl.BlockSpec(memory_space=pltpu.VMEM),
            scratch_shapes=[
                *[pltpu.VMEM(s, t) for s, t in zip(shapes, types)],
                vmem(tall, LANES),
                vmem(CHANNELS, tall, LANES),
                vmem(CHANNELS, tall, LANES),
                vmem(13, tall, LANES),
                vmem(CHANNELS, tall, LANES),
                vmem(2, ROWS, LANES),
                vmem(2, tall + 8, LANES),
                vmem(2, SENT, 8, LANES),
                vmem(2, SENT, 8, LANES),
                vmem(64, LANES),
                vmem(CHANNELS, 64, LANES),
                vmem(CHANNELS, 64, LANES),
                vmem(13, 64, LANES),
                vmem(CHANNELS, 64, LANES),
                vmem(6, 8, LANES),
                vmem(8, tall + 8, LANES),
                vmem(1, wide, LANES),
                vmem(1, wide, LANES),
                vmem(7, wide, LANES),
                vmem(1, wide, LANES),
                vmem(3, 8, LANES),
                vmem(2 * STEPS, tall, LANES),
                pltpu.SemaphoreType.DMA((6,)),
                pltpu.SemaphoreType.DMA((2,)),
                pltpu.SemaphoreType.DMA((2,)),
                pltpu.SemaphoreType.DMA((2,)),
                pltpu.SemaphoreType.DMA((2,)),
                pltpu.SemaphoreType.DMA((4,)),
                pltpu.SemaphoreType.DMA((4,)),
            ],
            compiler_params=pltpu.CompilerParams(
                collective_id=0, has_side_effects=True, vmem_limit_bytes=64900 * 1024
            ),
        )(*arrays)

    return jax.shard_map(
        local, mesh=mesh, in_specs=placed, out_specs=P(None, None, "lat", "lon"), check_vma=False
    )
```
